512 devices in a mesh: trow: 32 (over x_hi, z, core), tcol: 16 (over x_lo, y).
Axes of the slice: x: 4 (x_hi: 2, x_lo: 2; x = x_hi * 2 + x_lo), y: 8, z: 8, core: 2. Of those that a mesh axis runs over, the one named last changes fastest.
Arguments:
- start_modes: float32 [1, 32, 16, 512], P(None, 'trow', 'tcol'), may hold values from -0.018 to 0.018
- tiles: float32 [1, 32, 16, 1, 512, 512], P(None, 'trow', 'tcol'), may hold values from -0.046875 to 0.046875
- reach: int32 [1, 32], P(None, 'trow'), may hold values from 2 to 15
- weights: float32 [1, 32, 16, 32], P(None, 'trow', 'tcol'), may hold values from 0.5 to 2
Outputs:
- modes: float32 [1, 32, 16, 512], P(None, 'trow', 'tcol')
The draws below stay inside these ranges and needn't reach their ends.
Inputs may be any that keep to these rules, and one draw needn't show every extreme that they name: Tile row t uses the stored tiles of offsets 0 to reach of row t; tiles of larger offsets and those left of column 0 are ignored.
All inputs are finite; a program needn't handle non-finite values.
Results may differ from the reference program's by a relative error of at most 0.0001.
Values sent between devices are 32-bit elements; how exact they have to be, the bound alone decides.
A program may use at most 64 MiB of HBM per device.

```python
import math
import jax
import jax.numpy as jnp
from jax import lax

TB = 512
K = 16
BANDT = 16
RPD = 1
ITERS = 2
STATES = 16384
BPC = 1
SUB = 32
N_TROW = 32
N_TCOL = 16


def set_ends(entries, own_key, smallest, high):
    place = [jax.random.randint(jax.random.fold_in(own_key, axis), (), 0, length) for axis, length in enumerate(entries.shape)]
    longest = entries.shape.index(max(entries.shape))
    next_to = place[:longest] + [(place[longest] + 1) % entries.shape[longest]] + place[longest + 1:]
    return entries.at[tuple(place)].set(smallest).at[tuple(next_to)].set(high)


def block_levels(key, extent, pieces, smallest, top_value):
    def one(position, blocks):
        steps = jax.random.uniform(jax.random.fold_in(jax.random.fold_in(key, 6), position), (blocks,), jnp.float32, smallest / len(pieces), top_value / len(pieces))
        return jnp.repeat(jnp.exp(steps), extent[position] // blocks).reshape((-1,) + (1,) * (len(extent) - position - 1))

    factor_of = one(*pieces[0])
    for cut in pieces[1:]:
        factor_of = factor_of * one(*cut)
    return factor_of


def normal_values(own_key, dims, width, most, cuts=(), kind=jnp.bfloat16):
    entries = jax.random.normal(own_key, dims, jnp.float32) * width
    if len(cuts) > 0:
        entries = block_levels(own_key, dims, cuts, -0.22, 0.18) * entries
    return jnp.clip(entries, min=-most, max=most).astype(kind)


def setup_inputs(seed: int = 0) -> dict:
    key_of = jax.random.split(jax.random.key(seed), 5)
    start_modes = normal_values(key_of[0], (RPD, N_TROW, N_TCOL, SUB * K), 0.003, 0.018, ((1, 32), (2, 16)), jnp.float32)
    tiles = normal_values(key_of[1], (RPD, N_TROW, N_TCOL, BPC, TB, TB), (2 * TB * BANDT) ** -0.5, 0.046875, ((1, 32), (2, 16)), jnp.float32)
    reach = set_ends(jax.random.randint(key_of[2], (RPD, N_TROW), 2, 16), jax.random.fold_in(key_of[2], 1), 2, 15).astype(jnp.int32)
    weights = jnp.clip(jnp.exp(math.log(2.0) - 1.3862944 * jax.random.uniform(key_of[3], (RPD, N_TROW, N_TCOL, SUB), jnp.float32) ** block_levels(key_of[3], (RPD, N_TROW, N_TCOL, SUB), ((1, 32), (2, 16)), -0.2, 0.2)), 0.5, 2.0)
    return {"start_modes": start_modes, "tiles": tiles, "reach": reach, "weights": weights}


epsilon = 1e-06

def reference(start_modes, tiles, reach, weights):
    row_total = RPD * N_TROW
    row_ids = jnp.arange(RPD, dtype=jnp.int32)[:, None] * N_TROW + jnp.arange(N_TROW, dtype=jnp.int32)[None, :]
    trow_ids = jnp.arange(N_TROW, dtype=jnp.int32)[None, :, None, None]
    tcol_ids = jnp.arange(N_TCOL, dtype=jnp.int32)[None, None, :, None]
    block_ids = jnp.arange(BPC, dtype=jnp.int32)[None, None, None, :]
    offsets = (trow_ids - tcol_ids) % N_TCOL + N_TCOL * block_ids
    column_ids = row_ids[:, :, None, None] - offsets
    present = (offsets <= reach[:, :, None, None]) & (column_ids >= 0)
    keep_mask = present.astype(jnp.float32)
    safe_ids = jnp.maximum(column_ids, 0).astype(jnp.int32)
    pop_rows = weights.reshape(row_total, TB)
    mode_rows = start_modes.reshape(row_total, TB, K)
    for sweep in range(ITERS):
        scaled = mode_rows * pop_rows[:, :, None]
        far_rows = scaled[safe_ids] * keep_mask[..., None, None]
        forward = jnp.einsum('arcmpq,arcmqk->arpk', tiles, far_rows, precision=lax.Precision.HIGHEST)
        own_rows = scaled.reshape(RPD, N_TROW, TB, K)
        mirror = jnp.einsum('arcmpq,arpk->arcmqk', tiles, own_rows, precision=lax.Precision.HIGHEST)
        mirror = mirror * keep_mask[..., None, None]
        product = forward.reshape(row_total, TB, K)
        product = product.at[safe_ids.reshape(-1)].add(mirror.reshape(-1, TB, K))
        values = product * pop_rows[:, :, None]
        flat_rows = values.reshape(row_total * TB, K)
        gram_matrix = jnp.dot(flat_rows.T.astype(jnp.float32), flat_rows.astype(jnp.float32), precision=lax.Precision.HIGHEST, preferred_element_type=jnp.float32)
        gram_matrix = gram_matrix / STATES + epsilon * jnp.eye(K, dtype=jnp.float32)
        factor = jnp.linalg.cholesky(gram_matrix)
        solved = lax.linalg.triangular_solve(factor, flat_rows, left_side=False, lower=True, transpose_a=True)
        mode_rows = solved.reshape(row_total, TB, K)
    return mode_rows.reshape(RPD, N_TROW, N_TCOL, SUB * K)
```

```python
import functools

import jax
import jax.numpy as jnp
from jax import lax
from jax.experimental import pallas as pl
from jax.experimental.pallas import tpu as pltpu
from jax.sharding import PartitionSpec as P

K = 16
SUB = 32
EPS = 1e-06
F32 = jnp.float32
BF16 = jnp.bfloat16
MESH = pl.DeviceIdType.MESH
NT = (((1,), (1,)), ((), ()))
NN = (((1,), (0,)), ((), ()))


def iota(shape, axis):
    return lax.broadcasted_iota(jnp.int32, shape, axis)


def dot_half(a, b, dims):
    return lax.dot_general(a, b, dims, preferred_element_type=F32)


def swap_blocks(block):
    top, bottom = block[0:8], block[8:16]
    lane = iota((8, 128), 1)
    row = iota((8, 128), 0)
    low = lane < 64
    halves = (
        jnp.where(low, top, pltpu.roll(bottom, 64, 1)),
        jnp.where(low, pltpu.roll(top, 64, 1), bottom),
    )
    odd_lane = (lane // 32) % 2
    odd_row = row // 4
    done = []
    for half in halves:
        turned = pltpu.roll(half, 4, 0)
        moved = jnp.where(odd_lane == 1, pltpu.roll(turned, 32, 1), pltpu.roll(turned, 96, 1))
        done.append(jnp.where(odd_lane == odd_row, half, moved))
    return jnp.concatenate(done, axis=0)


def slab_to_vectors(slab):
    flat = slab.reshape(slab.shape[0] * 4, 128)
    return jnp.concatenate(
        [swap_blocks(flat[16 * i : 16 * i + 16]) for i in range(slab.shape[0] // 4)], axis=1
    )


def fold_lanes(value, shifts):
    for shift in shifts:
        value = value + pltpu.roll(value, shift, 1)
    return value


def rows_spread(packed):
    count = packed.shape[0]
    wide = jnp.concatenate(
        [jnp.broadcast_to(packed[a : a + 1], (8, 128)) for a in range(count)], axis=0
    )
    shape = (8 * count, 128)
    keep = iota(shape, 1) // 16 == iota(shape, 0) % 8
    return fold_lanes(jnp.where(keep, wide, 0.0), (64, 32, 16))


def rows_packed(spread):
    shape = spread.shape
    keep = iota(shape, 1) // 16 == iota(shape, 0) % 8
    held = jnp.where(keep, spread, 0.0)
    return jnp.concatenate(
        [jnp.sum(held[8 * a : 8 * a + 8], axis=0, keepdims=True) for a in range(shape[0] // 8)],
        axis=0,
    )


def split(value):
    high = value.astype(BF16)
    return high, (value - high.astype(F32)).astype(BF16)


def dot_split(a_parts, b_parts, dims):
    rows = a_parts[0].shape[0]
    both = dot_half(jnp.concatenate(a_parts, axis=0), b_parts[0], dims)
    return both[0:rows] + (both[rows:] + dot_half(a_parts[0], b_parts[1], dims))


def gram_spread(vectors):
    parts = split(vectors)
    return dot_split(parts, [jnp.concatenate([part] * 8, axis=0) for part in parts], NT)


def inverse_factor(gram):
    row = iota((8, 128), 0)
    tops = [jnp.broadcast_to(gram[0:8, k : k + 1], (8, 128)) for k in range(K)]
    bottoms = [jnp.broadcast_to(gram[8:16, k : k + 1], (8, 128)) for k in range(K)]
    unit = iota((8, 128), 1) % K
    right = [jnp.where(unit == row, 1.0, 0.0), jnp.where(unit == row + 8, 1.0, 0.0)]
    scale = [jnp.zeros((8, 128), F32), jnp.zeros((8, 128), F32)]
    for step in range(K):
        half, place = step // 8, step % 8
        here = (tops, bottoms)[half]
        pivot = here[step][place : place + 1]
        scale[half] = jnp.where(row == place, lax.rsqrt(pivot), scale[half])
        if step == K - 1:
            break
        inverse = 1.0 / pivot
        lines = [here[k][place : place + 1] for k in range(K)]
        right_line = right[half][place : place + 1]
        if step < 7:
            factor = jnp.where(row > place, tops[step] * inverse, 0.0)
            for k in range(step + 1, K):
                tops[k] = tops[k] - factor * lines[k]
            right[0] = right[0] - factor * right_line
        factor = bottoms[step] * inverse
        if half == 1:
            factor = jnp.where(row > place, factor, 0.0)
        for k in range(step + 1, K):
            bottoms[k] = bottoms[k] - factor * lines[k]
        right[1] = right[1] - factor * right_line
    return jnp.concatenate([right[0] * scale[0], right[1] * scale[1]], axis=0)


def far_first(count, period):
    return sorted(range(1, count), key=lambda o: (-min(o % period, period - o % period), o))


def kernel(
    n_row,
    n_col,
    states,
    x_hbm,
    tile_hbm,
    reach_hbm,
    weight_hbm,
    out_ref,
    x_ref,
    tile_ref,
    reach_ref,
    weight_ref,
    high_ref,
    low_ref,
    weight_row_ref,
    weight_parts_ref,
    chunk_weight_ref,
    z_ref,
    slab_ref,
    own_ref,
    far_ref,
    parts_ref,
    chunk_ref,
    wide_ref,
    gram_first_ref,
    gram_ref,
    gram_row_ref,
    gram_col_ref,
    result_ref,
    back_ref,
    load_sem,
    weight_sem,
    z_row_sem,
    z_col_sem,
    part_sem,
    gram_sem,
    back_sem,
    weight_sent,
    z_sent,
    own_sent,
    far_sent,
    gram_sent,
    back_sent,
):
    r = lax.axis_index("trow")
    c = lax.axis_index("tcol")
    chunks = n_col // 4
    home = lax.rem(r, n_col)
    d = lax.rem(r - c + n_row, n_col)
    j = lax.rem(r - d + n_row, n_row)
    off_diagonal = d != 0
    y_count = n_col // 2

    def owner(row, chunk):
        place = lax.rem(row, n_col)
        x_low = lax.rem(lax.div(place, y_count) + lax.div(chunk, 2), 2)
        return x_low * y_count + lax.rem(place + y_count - 1 + 2 * lax.rem(chunk, 2), y_count)

    owners = [owner(r, i) for i in range(chunks)]
    mine = sum(jnp.where(c == place, i, 0) for i, place in enumerate(owners))
    is_owner = functools.reduce(jnp.logical_or, [c == place for place in owners])
    not_owner = jnp.logical_not(is_owner)

    def push(source, target, sent, arrived, device):
        pltpu.make_async_remote_copy(
            src_ref=source,
            dst_ref=target,
            send_sem=sent,
            recv_sem=arrived,
            device_id=device,
            device_id_type=MESH,
        ).start()

    def wait_for(ref, sem):
        pltpu.make_async_copy(ref, ref, sem).wait()

    def user(o):
        return lax.rem(r + o, n_row), home

    def peer(o):
        return r, lax.rem(c + o, n_col)

    peers = far_first(n_col, y_count)
    users = far_first(n_col, n_col)

    loads = [
        pltpu.make_async_copy(source, target, load_sem.at[i])
        for i, (source, target) in enumerate(
            ((x_hbm, x_ref), (weight_hbm, weight_ref), (reach_hbm, reach_ref), (tile_hbm, tile_ref))
        )
    ]
    for load in loads:
        load.start()

    barrier = pltpu.get_barrier_semaphore()

    def greet(device):
        pl.semaphore_signal(barrier, inc=1, device_id=device, device_id_type=MESH)

    @pl.when(off_diagonal)
    def _():
        for o in range(n_col):
            greet((j, o))

    @pl.when(is_owner)
    def _():
        for o in users:
            greet(user(o))

    for o in peers:
        greet(peer(o))

    loads[0].wait()
    loads[1].wait()
    spread = rows_spread(x_ref[...])
    turned = jnp.transpose(jnp.concatenate([spread] * 4, axis=0))[0:16]
    weight = jnp.concatenate([weight_ref[...]] * 4, axis=1)
    scaled = jnp.where(iota((16, 128), 1) // 32 == iota((16, 128), 0) // 4, turned * weight, 0.0)
    eight = scaled[0:8] + scaled[8:16]
    piece = eight[0:4] + eight[4:8]
    z_ref[...] = piece
    slab_ref[0, c] = piece
    weight_row_ref[...] = weight

    pl.semaphore_wait(barrier, 2 * (n_col - 1) + jnp.where(off_diagonal, chunks, 0))
    for o in peers:
        push(z_ref, slab_ref.at[0, c], z_sent.at[0], z_row_sem.at[0], peer(o))
    for o in users:
        push(z_ref, slab_ref.at[1, c], z_sent.at[0], z_col_sem.at[0], user(o))

    group, slot = lax.div(c, 4), lax.rem(c, 4)
    keeper = owner(r, group)

    @pl.when(c == keeper)
    def _():
        weight_parts_ref[slot] = weight

    @pl.when(c != keeper)
    def _():
        push(weight_row_ref, weight_parts_ref.at[slot], weight_sent, weight_sem, (r, keeper))

    loads[2].wait()
    loads[3].wait()
    keep = jnp.where(d <= reach_ref[...], 1.0, 0.0) * jnp.where(r >= d, 1.0, 0.0)
    tile = tile_ref[...] * keep
    high_ref[0], low_ref[0] = split(tile)
    high_ref[1], low_ref[1] = split(jnp.transpose(tile))
    lone = jnp.where(off_diagonal, 0.0, 1.0)

    def multiply(sweep, near, far_vectors):
        mirror = dot_split(split(near), (high_ref[0], low_ref[0]), NN)
        for i in range(chunks):
            far_ref[sweep, i] = mirror[:, 128 * i : 128 * i + 128]

        @pl.when(off_diagonal)
        def _():
            for turn in range(chunks):
                i = lax.rem(d + turn, chunks)
                push(
                    far_ref.at[sweep, i],
                    parts_ref.at[sweep, n_col - 2 + d],
                    far_sent.at[sweep],
                    part_sem.at[sweep],
                    (j, owner(j, i)),
                )

        forward = dot_split(split(far_vectors()), (high_ref[1], low_ref[1]), NN) + lone * mirror
        for i in range(chunks):
            own_ref[sweep, i] = forward[:, 128 * i : 128 * i + 128]
        for turn in range(chunks):
            i = lax.rem(c + turn, chunks)
            place = owner(r, i)

            @pl.when(c != place)
            def _():
                push(
                    own_ref.at[sweep, i],
                    parts_ref.at[sweep, lax.rem(place - c + n_col, n_col) - 1],
                    own_sent.at[sweep],
                    part_sem.at[sweep],
                    (r, place),
                )

    def total(sweep):
        wait_for(parts_ref.at[sweep], part_sem.at[sweep])
        return own_ref[sweep, mine] + jnp.sum(parts_ref[sweep], axis=0)

    side = jnp.where(off_diagonal, 1, 0)

    wait_for(slab_ref.at[0, pl.ds(0, n_col - 1)], z_row_sem.at[0])

    def far_pieces():
        @pl.when(off_diagonal)
        def _():
            wait_for(slab_ref.at[1], z_col_sem.at[0])

        return slab_to_vectors(slab_ref[side])

    multiply(0, slab_to_vectors(slab_ref[0]), far_pieces)

    @pl.when(is_owner)
    def _():
        inside = mine == group

        @pl.when(inside)
        def _():
            wait_for(weight_parts_ref.at[pl.ds(0, 3)], weight_sem)

        @pl.when(jnp.logical_not(inside))
        def _():
            wait_for(weight_parts_ref, weight_sem)

        lane = iota((1, 128), 1) // SUB
        chunk_weight = sum(jnp.where(lane == i, weight_parts_ref[i], 0.0) for i in range(4))
        chunk_weight_ref[...] = chunk_weight
        values = total(0) * chunk_weight
        scaled = values * chunk_weight
        chunk_ref[...] = scaled
        wide_ref[0, mine] = scaled
        for o in peers:
            push(chunk_ref, wide_ref.at[0, mine], z_sent.at[1], z_row_sem.at[1], peer(o))
        for o in users:
            push(chunk_ref, wide_ref.at[1, mine], z_sent.at[1], z_col_sem.at[1], user(o))
        gram_first_ref[...] = gram_spread(values)
        if chunks > 1:
            wait_for(wide_ref.at[0, pl.ds(0, chunks - 1)], z_row_sem.at[1])

    @pl.when(not_owner)
    def _():
        wait_for(wide_ref.at[0], z_row_sem.at[1])

    def far_chunks():
        @pl.when(off_diagonal)
        def _():
            wait_for(wide_ref.at[1], z_col_sem.at[1])

        return jnp.concatenate([wide_ref[side, i] for i in range(chunks)], axis=1)

    multiply(1, jnp.concatenate([wide_ref[0, i] for i in range(chunks)], axis=1), far_chunks)

    @pl.when(is_owner)
    def _():
        values = total(1) * chunk_weight_ref[...]
        gram = rows_packed(gram_spread(values) + EPS * gram_first_ref[...])
        gram_ref[0] = gram
        gram_row_ref[mine] = gram
        for o in peers:
            push(gram_ref.at[0], gram_row_ref.at[mine], gram_sent.at[0], gram_sem.at[0], peer(o))
        turned = jnp.transpose(jnp.concatenate([values] * 8, axis=0))
        result_ref[...] = rows_packed(turned).reshape(4, 4, 128)
        for i in range(4):
            place = 4 * mine + i

            @pl.when(c == place)
            def _():
                back_ref[...] = result_ref[i]

            @pl.when(c != place)
            def _():
                push(result_ref.at[i], back_ref, back_sent, back_sem, (r, place))

        if chunks > 1:
            wait_for(gram_row_ref.at[pl.ds(0, chunks - 1)], gram_sem.at[0])

    @pl.when(not_owner)
    def _():
        wait_for(gram_row_ref, gram_sem.at[0])

    gram_own = jnp.sum(gram_row_ref[...], axis=0)
    gram_ref[1] = gram_own
    for o in far_first(n_row, n_col):
        row = lax.rem(r + o, n_row)
        push(gram_ref.at[1], gram_col_ref.at[o - 1], gram_sent.at[1], gram_sem.at[1], (row, c))

    @pl.when(c != keeper)
    def _():
        wait_for(back_ref, back_sem)

    back = split(jnp.concatenate([back_ref[...]] * 4, axis=0))
    wait_for(gram_col_ref, gram_sem.at[1])
    gram = rows_spread(gram_own + jnp.sum(gram_col_ref[...], axis=0))
    diagonal = jnp.where(iota((16, 128), 1) % K == iota((16, 128), 0), EPS * EPS, 0.0)
    solver = inverse_factor(gram * (1.0 / states) + diagonal)
    wide = jnp.concatenate([solver] * 8, axis=0)
    wide = jnp.where(iota((128, 128), 0) // K == iota((128, 128), 1) // K, wide, 0.0)
    out_ref[...] = dot_split(back, split(wide), NT)[0:4]

    wait_for(slab_ref.at[:, pl.ds(0, n_col - 1)], z_sent.at[0])
    wait_for(gram_col_ref, gram_sent.at[1])

    @pl.when(c != keeper)
    def _():
        wait_for(weight_row_ref, weight_sent)

    for sweep in range(2):

        @pl.when(off_diagonal)
        def _():
            wait_for(far_ref.at[sweep], far_sent.at[sweep])

        @pl.when(is_owner)
        def _():
            if chunks > 1:
                wait_for(own_ref.at[sweep, pl.ds(0, chunks - 1)], own_sent.at[sweep])

        @pl.when(not_owner)
        def _():
            wait_for(own_ref.at[sweep], own_sent.at[sweep])

    @pl.when(is_owner)
    def _():
        wait_for(parts_ref.at[0], z_sent.at[1])
        wait_for(gram_col_ref.at[pl.ds(0, n_col - 1)], gram_sent.at[0])

        @pl.when(mine == group)
        def _():
            wait_for(result_ref.at[pl.ds(0, 3)], back_sent)

        @pl.when(mine != group)
        def _():
            wait_for(result_ref, back_sent)


def local(start_modes, tiles, reach, weights, n_row, n_col):
    width = tiles.shape[-1]
    chunks = n_col // 4
    dma = pltpu.SemaphoreType.DMA
    out = pl.pallas_call(
        functools.partial(kernel, n_row, n_col, n_row * width),
        out_shape=pltpu.VMEM((4, 128), F32),
        in_specs=[pl.BlockSpec(memory_space=pltpu.HBM)] * 4,
        out_specs=pl.BlockSpec(memory_space=pltpu.VMEM),
        scratch_shapes=[
            pltpu.VMEM((4, 128), F32),
            pltpu.VMEM((width, width), F32),
            pltpu.VMEM((1, 1), jnp.int32),
            pltpu.VMEM((1, SUB), F32),
            pltpu.VMEM((2, width, width), BF16),
            pltpu.VMEM((2, width, width), BF16),
            pltpu.VMEM((1, 128), F32),
            pltpu.VMEM((4, 1, 128), F32),
            pltpu.VMEM((1, 128), F32),
            pltpu.VMEM((4, 128), F32),
            pltpu.VMEM((2, n_col, 4, 128), F32),
            pltpu.VMEM((2, chunks, K, 128), F32),
            pltpu.VMEM((2, chunks, K, 128), F32),
            pltpu.VMEM((2, 2 * (n_col - 1), K, 128), F32),
            pltpu.VMEM((K, 128), F32),
            pltpu.VMEM((2, chunks, K, 128), F32),
            pltpu.VMEM((K, 128), F32),
            pltpu.VMEM((2, 2, 128), F32),
            pltpu.VMEM((chunks, 2, 128), F32),
            pltpu.VMEM((n_row - 1, 2, 128), F32),
            pltpu.VMEM((4, 4, 128), F32),
            pltpu.VMEM((4, 128), F32),
            dma((4,)),
            dma(()),
            dma((2,)),
            dma((2,)),
            dma((2,)),
            dma((2,)),
            dma(()),
            dma(()),
            dma((2,)),
            dma((2,)),
            dma((2,)),
            dma((2,)),
            dma(()),
        ],
        compiler_params=pltpu.CompilerParams(
            collective_id=0, has_side_effects=True, vmem_limit_bytes=60 * 1024 * 1024
        ),
    )(
        start_modes.reshape(4, 128),
        tiles.reshape(width, width),
        reach,
        weights.reshape(1, SUB),
    )
    return out.reshape(start_modes.shape)


def solution(mesh):
    return jax.shard_map(
        functools.partial(local, n_row=mesh.shape["trow"], n_col=mesh.shape["tcol"]),
        mesh=mesh,
        in_specs=(
            P(None, "trow", "tcol", None),
            P(None, "trow", "tcol", None, None, None),
            P(None, "trow"),
            P(None, "trow", "tcol", None),
        ),
        out_specs=P(None, "trow", "tcol", None),
        check_vma=False,
    )
```

```python
import functools

import jax
import jax.numpy as jnp
from jax import lax
from jax.experimental import pallas as pl
from jax.experimental.pallas import tpu as pltpu
from jax.sharding import PartitionSpec as P

K = 16
SUB = 32
EPS = 1e-06
F32 = jnp.float32
BF16 = jnp.bfloat16
MESH = pl.DeviceIdType.MESH
NT = (((1,), (1,)), ((), ()))
NN = (((1,), (0,)), ((), ()))


def iota(shape, axis):
    return lax.broadcasted_iota(jnp.int32, shape, axis)


def dot_half(a, b, dims):
    return lax.dot_general(a, b, dims, preferred_element_type=F32)


def swap_blocks(block):
    top, bottom = block[0:8], block[8:16]
    lane = iota((8, 128), 1)
    row = iota((8, 128), 0)
    low = lane < 64
    halves = (
        jnp.where(low, top, pltpu.roll(bottom, 64, 1)),
        jnp.where(low, pltpu.roll(top, 64, 1), bottom),
    )
    odd_lane = (lane // 32) % 2
    odd_row = row // 4
    done = []
    for half in halves:
        turned = pltpu.roll(half, 4, 0)
        moved = jnp.where(odd_lane == 1, pltpu.roll(turned, 32, 1), pltpu.roll(turned, 96, 1))
        done.append(jnp.where(odd_lane == odd_row, half, moved))
    return jnp.concatenate(done, axis=0)


def slab_to_vectors(slab):
    flat = slab.reshape(slab.shape[0] * 4, 128)
    return jnp.concatenate(
        [swap_blocks(flat[16 * i : 16 * i + 16]) for i in range(slab.shape[0] // 4)], axis=1
    )


def fold_lanes(value, shifts):
    for shift in shifts:
        value = value + pltpu.roll(value, shift, 1)
    return value


def rows_spread(packed):
    count = packed.shape[0]
    wide = jnp.concatenate(
        [jnp.broadcast_to(packed[a : a + 1], (8, 128)) for a in range(count)], axis=0
    )
    shape = (8 * count, 128)
    keep = iota(shape, 1) // 16 == iota(shape, 0) % 8
    return fold_lanes(jnp.where(keep, wide, 0.0), (64, 32, 16))


def rows_packed(spread):
    shape = spread.shape
    keep = iota(shape, 1) // 16 == iota(shape, 0) % 8
    held = jnp.where(keep, spread, 0.0)
    return jnp.concatenate(
        [jnp.sum(held[8 * a : 8 * a + 8], axis=0, keepdims=True) for a in range(shape[0] // 8)],
        axis=0,
    )


def split(value):
    high = value.astype(BF16)
    return high, (value - high.astype(F32)).astype(BF16)


def dot_split(a_parts, b_parts, dims):
    rows = a_parts[0].shape[0]
    both = dot_half(jnp.concatenate(a_parts, axis=0), b_parts[0], dims)
    return both[0:rows] + (both[rows:] + dot_half(a_parts[0], b_parts[1], dims))


def gram_spread(vectors):
    parts = split(vectors)
    return dot_split(parts, [jnp.concatenate([part] * 8, axis=0) for part in parts], NT)


def inverse_factor(gram):
    row = iota((8, 128), 0)
    tops = [jnp.broadcast_to(gram[0:8, k : k + 1], (8, 128)) for k in range(K)]
    bottoms = [jnp.broadcast_to(gram[8:16, k : k + 1], (8, 128)) for k in range(K)]
    unit = iota((8, 128), 1) % K
    right = [jnp.where(unit == row, 1.0, 0.0), jnp.where(unit == row + 8, 1.0, 0.0)]
    scale = [jnp.zeros((8, 128), F32), jnp.zeros((8, 128), F32)]
    for step in range(K):
        half, place = step // 8, step % 8
        here = (tops, bottoms)[half]
        pivot = here[step][place : place + 1]
        scale[half] = jnp.where(row == place, lax.rsqrt(pivot), scale[half])
        if step == K - 1:
            break
        inverse = 1.0 / pivot
        lines = [here[k][place : place + 1] for k in range(K)]
        right_line = right[half][place : place + 1]
        if step < 7:
            factor = jnp.where(row > place, tops[step] * inverse, 0.0)
            for k in range(step + 1, K):
                tops[k] = tops[k] - factor * lines[k]
            right[0] = right[0] - factor * right_line
        factor = bottoms[step] * inverse
        if half == 1:
            factor = jnp.where(row > place, factor, 0.0)
        for k in range(step + 1, K):
            bottoms[k] = bottoms[k] - factor * lines[k]
        right[1] = right[1] - factor * right_line
    return jnp.concatenate([right[0] * scale[0], right[1] * scale[1]], axis=0)


def far_first(count, period):
    return sorted(range(1, count), key=lambda o: (-min(o % period, period - o % period), o))


def kernel(
    n_row,
    n_col,
    states,
    x_hbm,
    tile_hbm,
    reach_hbm,
    weight_hbm,
    out_ref,
    x_ref,
    tile_ref,
    reach_ref,
    weight_ref,
    high_ref,
    low_ref,
    weight_row_ref,
    weight_parts_ref,
    chunk_weight_ref,
    z_ref,
    slab_ref,
    own_ref,
    far_ref,
    parts_ref,
    chunk_ref,
    wide_ref,
    gram_first_ref,
    gram_ref,
    gram_row_ref,
    gram_col_ref,
    result_ref,
    back_ref,
    load_sem,
    weight_sem,
    z_row_sem,
    z_col_sem,
    part_sem,
    gram_sem,
    back_sem,
    weight_sent,
    z_sent,
    own_sent,
    far_sent,
    gram_sent,
    back_sent,
):
    r = lax.axis_index("trow")
    c = lax.axis_index("tcol")
    chunks = n_col // 4
    home = lax.rem(r, n_col)
    d = lax.rem(r - c + n_row, n_col)
    j = lax.rem(r - d + n_row, n_row)
    off_diagonal = d != 0
    y_count = n_col // 2

    def owner(row, chunk):
        place = lax.rem(row, n_col)
        x_low = lax.rem(lax.div(place, y_count) + lax.div(chunk, 2), 2)
        return x_low * y_count + lax.rem(place + y_count - 1 + 2 * lax.rem(chunk, 2), y_count)

    owners = [owner(r, i) for i in range(chunks)]
    mine = sum(jnp.where(c == place, i, 0) for i, place in enumerate(owners))
    is_owner = functools.reduce(jnp.logical_or, [c == place for place in owners])
    not_owner = jnp.logical_not(is_owner)

    def push(source, target, sent, arrived, device):
        pltpu.make_async_remote_copy(
            src_ref=source,
            dst_ref=target,
            send_sem=sent,
            recv_sem=arrived,
            device_id=device,
            device_id_type=MESH,
        ).start()

    def wait_for(ref, sem):
        pltpu.make_async_copy(ref, ref, sem).wait()

    def user(o):
        return lax.rem(r + o, n_row), home

    def peer(o):
        return r, lax.rem(c + o, n_col)

    peers = far_first(n_col, y_count)
    users = far_first(n_col, n_col)

    loads = [
        pltpu.make_async_copy(source, target, load_sem.at[i])
        for i, (source, target) in enumerate(
            ((x_hbm, x_ref), (weight_hbm, weight_ref), (reach_hbm, reach_ref), (tile_hbm, tile_ref))
        )
    ]
    for load in loads:
        load.start()

    barrier = pltpu.get_barrier_semaphore()

    def greet(device):
        pl.semaphore_signal(barrier, inc=1, device_id=device, device_id_type=MESH)

    @pl.when(off_diagonal)
    def _():
        for o in range(n_col):
            greet((j, o))

    @pl.when(is_owner)
    def _():
        for o in users:
            greet(user(o))

    for o in peers:
        greet(peer(o))

    loads[0].wait()
    loads[1].wait()
    spread = rows_spread(x_ref[...])
    turned = jnp.transpose(jnp.concatenate([spread] * 4, axis=0))[0:16]
    weight = jnp.concatenate([weight_ref[...]] * 4, axis=1)
    scaled = jnp.where(iota((16, 128), 1) // 32 == iota((16, 128), 0) // 4, turned * weight, 0.0)
    eight = scaled[0:8] + scaled[8:16]
    piece = eight[0:4] + eight[4:8]
    z_ref[...] = piece
    slab_ref[0, c] = piece
    weight_row_ref[...] = weight

    pl.semaphore_wait(barrier, 2 * (n_col - 1) + jnp.where(off_diagonal, chunks, 0))
    for o in users:
        push(z_ref, slab_ref.at[1, c], z_sent.at[0], z_col_sem.at[0], user(o))
    for o in peers:
        push(z_ref, slab_ref.at[0, c], z_sent.at[0], z_row_sem.at[0], peer(o))

    group, slot = lax.div(c, 4), lax.rem(c, 4)
    keeper = owner(r, group)

    @pl.when(c == keeper)
    def _():
        weight_parts_ref[slot] = weight

    @pl.when(c != keeper)
    def _():
        push(weight_row_ref, weight_parts_ref.at[slot], weight_sent, weight_sem, (r, keeper))

    loads[2].wait()
    loads[3].wait()
    keep = jnp.where(d <= reach_ref[...], 1.0, 0.0) * jnp.where(r >= d, 1.0, 0.0)
    tile = tile_ref[...] * keep
    high_ref[0], low_ref[0] = split(tile)
    high_ref[1], low_ref[1] = split(jnp.transpose(tile))
    lone = jnp.where(off_diagonal, 0.0, 1.0)

    def multiply(sweep, near, far_vectors):
        mirror = dot_split(split(near), (high_ref[0], low_ref[0]), NN)
        for i in range(chunks):
            far_ref[sweep, i] = mirror[:, 128 * i : 128 * i + 128]

        @pl.when(off_diagonal)
        def _():
            for turn in range(chunks):
                i = lax.rem(d + turn, chunks)
                push(
                    far_ref.at[sweep, i],
                    parts_ref.at[sweep, n_col - 2 + d],
                    far_sent.at[sweep],
                    part_sem.at[sweep],
                    (j, owner(j, i)),
                )

        forward = dot_split(split(far_vectors()), (high_ref[1], low_ref[1]), NN) + lone * mirror
        for i in range(chunks):
            own_ref[sweep, i] = forward[:, 128 * i : 128 * i + 128]
        for turn in range(chunks):
            i = lax.rem(c + turn, chunks)
            place = owner(r, i)

            @pl.when(c != place)
            def _():
                push(
                    own_ref.at[sweep, i],
                    parts_ref.at[sweep, lax.rem(place - c + n_col, n_col) - 1],
                    own_sent.at[sweep],
                    part_sem.at[sweep],
                    (r, place),
                )

    def total(sweep):
        wait_for(parts_ref.at[sweep], part_sem.at[sweep])
        return own_ref[sweep, mine] + jnp.sum(parts_ref[sweep], axis=0)

    side = jnp.where(off_diagonal, 1, 0)

    wait_for(slab_ref.at[0, pl.ds(0, n_col - 1)], z_row_sem.at[0])

    def far_pieces():
        @pl.when(off_diagonal)
        def _():
            wait_for(slab_ref.at[1], z_col_sem.at[0])

        return slab_to_vectors(slab_ref[side])

    multiply(0, slab_to_vectors(slab_ref[0]), far_pieces)

    @pl.when(is_owner)
    def _():
        inside = mine == group

        @pl.when(inside)
        def _():
            wait_for(weight_parts_ref.at[pl.ds(0, 3)], weight_sem)

        @pl.when(jnp.logical_not(inside))
        def _():
            wait_for(weight_parts_ref, weight_sem)

        lane = iota((1, 128), 1) // SUB
        chunk_weight = sum(jnp.where(lane == i, weight_parts_ref[i], 0.0) for i in range(4))
        chunk_weight_ref[...] = chunk_weight
        values = total(0) * chunk_weight
        scaled = values * chunk_weight
        chunk_ref[...] = scaled
        wide_ref[0, mine] = scaled
        for o in peers:
            push(chunk_ref, wide_ref.at[0, mine], z_sent.at[1], z_row_sem.at[1], peer(o))
        for o in users:
            push(chunk_ref, wide_ref.at[1, mine], z_sent.at[1], z_col_sem.at[1], user(o))
        gram_first_ref[...] = gram_spread(values)
        if chunks > 1:
            wait_for(wide_ref.at[0, pl.ds(0, chunks - 1)], z_row_sem.at[1])

    @pl.when(not_owner)
    def _():
        wait_for(wide_ref.at[0], z_row_sem.at[1])

    def far_chunks():
        @pl.when(off_diagonal)
        def _():
            wait_for(wide_ref.at[1], z_col_sem.at[1])

        return jnp.concatenate([wide_ref[side, i] for i in range(chunks)], axis=1)

    multiply(1, jnp.concatenate([wide_ref[0, i] for i in range(chunks)], axis=1), far_chunks)

    @pl.when(is_owner)
    def _():
        values = total(1) * chunk_weight_ref[...]
        gram = rows_packed(gram_spread(values) + EPS * gram_first_ref[...])
        gram_ref[0] = gram
        gram_row_ref[mine] = gram
        for o in peers:
            push(gram_ref.at[0], gram_row_ref.at[mine], gram_sent.at[0], gram_sem.at[0], peer(o))
        turned = jnp.transpose(jnp.concatenate([values] * 8, axis=0))
        result_ref[...] = rows_packed(turned).reshape(4, 4, 128)
        for i in range(4):
            place = 4 * mine + i

            @pl.when(c == place)
            def _():
                back_ref[...] = result_ref[i]

            @pl.when(c != place)
            def _():
                push(result_ref.at[i], back_ref, back_sent, back_sem, (r, place))

        if chunks > 1:
            wait_for(gram_row_ref.at[pl.ds(0, chunks - 1)], gram_sem.at[0])

    @pl.when(not_owner)
    def _():
        wait_for(gram_row_ref, gram_sem.at[0])

    gram_own = jnp.sum(gram_row_ref[...], axis=0)
    gram_ref[1] = gram_own
    for o in far_first(n_row, n_col):
        row = lax.rem(r + o, n_row)
        push(gram_ref.at[1], gram_col_ref.at[o - 1], gram_sent.at[1], gram_sem.at[1], (row, c))

    @pl.when(c != keeper)
    def _():
        wait_for(back_ref, back_sem)

    back = split(jnp.concatenate([back_ref[...]] * 4, axis=0))
    wait_for(gram_col_ref, gram_sem.at[1])
    gram = rows_spread(gram_own + jnp.sum(gram_col_ref[...], axis=0))
    diagonal = jnp.where(iota((16, 128), 1) % K == iota((16, 128), 0), EPS * EPS, 0.0)
    solver = inverse_factor(gram * (1.0 / states) + diagonal)
    wide = jnp.concatenate([solver] * 8, axis=0)
    wide = jnp.where(iota((128, 128), 0) // K == iota((128, 128), 1) // K, wide, 0.0)
    out_ref[...] = dot_split(back, split(wide), NT)[0:4]

    wait_for(slab_ref.at[:, pl.ds(0, n_col - 1)], z_sent.at[0])
    wait_for(gram_col_ref, gram_sent.at[1])

    @pl.when(c != keeper)
    def _():
        wait_for(weight_row_ref, weight_sent)

    for sweep in range(2):

        @pl.when(off_diagonal)
        def _():
            wait_for(far_ref.at[sweep], far_sent.at[sweep])

        @pl.when(is_owner)
        def _():
            if chunks > 1:
                wait_for(own_ref.at[sweep, pl.ds(0, chunks - 1)], own_sent.at[sweep])

        @pl.when(not_owner)
        def _():
            wait_for(own_ref.at[sweep], own_sent.at[sweep])

    @pl.when(is_owner)
    def _():
        wait_for(parts_ref.at[0], z_sent.at[1])
        wait_for(gram_col_ref.at[pl.ds(0, n_col - 1)], gram_sent.at[0])

        @pl.when(mine == group)
        def _():
            wait_for(result_ref.at[pl.ds(0, 3)], back_sent)

        @pl.when(mine != group)
        def _():
            wait_for(result_ref, back_sent)


def local(start_modes, tiles, reach, weights, n_row, n_col):
    width = tiles.shape[-1]
    chunks = n_col // 4
    dma = pltpu.SemaphoreType.DMA
    out = pl.pallas_call(
        functools.partial(kernel, n_row, n_col, n_row * width),
        out_shape=pltpu.VMEM((4, 128), F32),
        in_specs=[pl.BlockSpec(memory_space=pltpu.HBM)] * 4,
        out_specs=pl.BlockSpec(memory_space=pltpu.VMEM),
        scratch_shapes=[
            pltpu.VMEM((4, 128), F32),
            pltpu.VMEM((width, width), F32),
            pltpu.VMEM((1, 1), jnp.int32),
            pltpu.VMEM((1, SUB), F32),
            pltpu.VMEM((2, width, width), BF16),
            pltpu.VMEM((2, width, width), BF16),
            pltpu.VMEM((1, 128), F32),
            pltpu.VMEM((4, 1, 128), F32),
            pltpu.VMEM((1, 128), F32),
            pltpu.VMEM((4, 128), F32),
            pltpu.VMEM((2, n_col, 4, 128), F32),
            pltpu.VMEM((2, chunks, K, 128), F32),
            pltpu.VMEM((2, chunks, K, 128), F32),
            pltpu.VMEM((2, 2 * (n_col - 1), K, 128), F32),
            pltpu.VMEM((K, 128), F32),
            pltpu.VMEM((2, chunks, K, 128), F32),
            pltpu.VMEM((K, 128), F32),
            pltpu.VMEM((2, 2, 128), F32),
            pltpu.VMEM((chunks, 2, 128), F32),
            pltpu.VMEM((n_row - 1, 2, 128), F32),
            pltpu.VMEM((4, 4, 128), F32),
            pltpu.VMEM((4, 128), F32),
            dma((4,)),
            dma(()),
            dma((2,)),
            dma((2,)),
            dma((2,)),
            dma((2,)),
            dma(()),
            dma(()),
            dma((2,)),
            dma((2,)),
            dma((2,)),
            dma((2,)),
            dma(()),
        ],
        compiler_params=pltpu.CompilerParams(
            collective_id=0, has_side_effects=True, vmem_limit_bytes=60 * 1024 * 1024
        ),
    )(
        start_modes.reshape(4, 128),
        tiles.reshape(width, width),
        reach,
        weights.reshape(1, SUB),
    )
    return out.reshape(start_modes.shape)


def solution(mesh):
    return jax.shard_map(
        functools.partial(local, n_row=mesh.shape["trow"], n_col=mesh.shape["tcol"]),
        mesh=mesh,
        in_specs=(
            P(None, "trow", "tcol", None),
            P(None, "trow", "tcol", None, None, None),
            P(None, "trow"),
            P(None, "trow", "tcol", None),
        ),
        out_specs=P(None, "trow", "tcol", None),
        check_vma=False,
    )
```

```python
import functools

import jax
import jax.numpy as jnp
from jax import lax
from jax.experimental import pallas as pl
from jax.experimental.pallas import tpu as pltpu
from jax.sharding import PartitionSpec as P

K = 16
SUB = 32
EPS = 1e-06
F32 = jnp.float32
BF16 = jnp.bfloat16
MESH = pl.DeviceIdType.MESH
NT = (((1,), (1,)), ((), ()))
NN = (((1,), (0,)), ((), ()))


def iota(shape, axis):
    return lax.broadcasted_iota(jnp.int32, shape, axis)


def dot_half(a, b, dims):
    return lax.dot_general(a, b, dims, preferred_element_type=F32)


def swap_blocks(block):
    top, bottom = block[0:8], block[8:16]
    lane = iota((8, 128), 1)
    row = iota((8, 128), 0)
    low = lane < 64
    halves = (
        jnp.where(low, top, pltpu.roll(bottom, 64, 1)),
        jnp.where(low, pltpu.roll(top, 64, 1), bottom),
    )
    odd_lane = (lane // 32) % 2
    odd_row = row // 4
    done = []
    for half in halves:
        turned = pltpu.roll(half, 4, 0)
        moved = jnp.where(odd_lane == 1, pltpu.roll(turned, 32, 1), pltpu.roll(turned, 96, 1))
        done.append(jnp.where(odd_lane == odd_row, half, moved))
    return jnp.concatenate(done, axis=0)


def slab_to_vectors(slab):
    flat = slab.reshape(slab.shape[0] * 4, 128)
    return jnp.concatenate(
        [swap_blocks(flat[16 * i : 16 * i + 16]) for i in range(slab.shape[0] // 4)], axis=1
    )


def fold_lanes(value, shifts):
    for shift in shifts:
        value = value + pltpu.roll(value, shift, 1)
    return value


def rows_spread(packed):
    count = packed.shape[0]
    wide = jnp.concatenate(
        [jnp.broadcast_to(packed[a : a + 1], (8, 128)) for a in range(count)], axis=0
    )
    shape = (8 * count, 128)
    keep = iota(shape, 1) // 16 == iota(shape, 0) % 8
    return fold_lanes(jnp.where(keep, wide, 0.0), (64, 32, 16))


def rows_packed(spread):
    shape = spread.shape
    keep = iota(shape, 1) // 16 == iota(shape, 0) % 8
    held = jnp.where(keep, spread, 0.0)
    return jnp.concatenate(
        [jnp.sum(held[8 * a : 8 * a + 8], axis=0, keepdims=True) for a in range(shape[0] // 8)],
        axis=0,
    )


def split(value):
    high = value.astype(BF16)
    return high, (value - high.astype(F32)).astype(BF16)


def dot_split(a_parts, b_parts, dims):
    rows = a_parts[0].shape[0]
    both = dot_half(jnp.concatenate(a_parts, axis=0), b_parts[0], dims)
    return both[0:rows] + (both[rows:] + dot_half(a_parts[0], b_parts[1], dims))


def gram_spread(vectors):
    parts = split(vectors)
    return dot_split(parts, [jnp.concatenate([part] * 8, axis=0) for part in parts], NT)


def inverse_factor(gram):
    row = iota((8, 128), 0)
    tops = [jnp.broadcast_to(gram[0:8, k : k + 1], (8, 128)) for k in range(K)]
    bottoms = [jnp.broadcast_to(gram[8:16, k : k + 1], (8, 128)) for k in range(K)]
    unit = iota((8, 128), 1) % K
    right = [jnp.where(unit == row, 1.0, 0.0), jnp.where(unit == row + 8, 1.0, 0.0)]
    scale = [jnp.zeros((8, 128), F32), jnp.zeros((8, 128), F32)]
    for step in range(K):
        half, place = step // 8, step % 8
        here = (tops, bottoms)[half]
        pivot = here[step][place : place + 1]
        scale[half] = jnp.where(row == place, lax.rsqrt(pivot), scale[half])
        if step == K - 1:
            break
        inverse = 1.0 / pivot
        lines = [here[k][place : place + 1] for k in range(K)]
        right_line = right[half][place : place + 1]
        if step < 7:
            factor = jnp.where(row > place, tops[step] * inverse, 0.0)
            for k in range(step + 1, K):
                tops[k] = tops[k] - factor * lines[k]
            right[0] = right[0] - factor * right_line
        factor = bottoms[step] * inverse
        if half == 1:
            factor = jnp.where(row > place, factor, 0.0)
        for k in range(step + 1, K):
            bottoms[k] = bottoms[k] - factor * lines[k]
        right[1] = right[1] - factor * right_line
    return jnp.concatenate([right[0] * scale[0], right[1] * scale[1]], axis=0)


def far_first(count, period):
    return sorted(range(1, count), key=lambda o: (-min(o % period, period - o % period), o))


def kernel(
    n_row,
    n_col,
    states,
    x_hbm,
    tile_hbm,
    reach_hbm,
    weight_hbm,
    out_ref,
    x_ref,
    tile_ref,
    reach_ref,
    weight_ref,
    high_ref,
    low_ref,
    weight_row_ref,
    weight_parts_ref,
    chunk_weight_ref,
    z_ref,
    slab_ref,
    own_ref,
    far_ref,
    parts_ref,
    chunk_ref,
    wide_ref,
    gram_first_ref,
    gram_ref,
    gram_row_ref,
    gram_col_ref,
    result_ref,
    back_ref,
    load_sem,
    weight_sem,
    z_row_sem,
    z_first_sem,
    z_col_sem,
    part_sem,
    gram_sem,
    back_sem,
    weight_sent,
    z_sent,
    own_sent,
    far_sent,
    gram_sent,
    back_sent,
):
    r = lax.axis_index("trow")
    c = lax.axis_index("tcol")
    chunks = n_col // 4
    home = lax.rem(r, n_col)
    d = lax.rem(r - c + n_row, n_col)
    j = lax.rem(r - d + n_row, n_row)
    off_diagonal = d != 0
    y_count = n_col // 2

    def owner(row, chunk):
        place = lax.rem(row, n_col)
        x_low = lax.rem(lax.div(place, y_count) + lax.div(chunk, 2), 2)
        return x_low * y_count + lax.rem(place + y_count - 1 + 2 * lax.rem(chunk, 2), y_count)

    owners = [owner(r, i) for i in range(chunks)]
    mine = sum(jnp.where(c == place, i, 0) for i, place in enumerate(owners))
    is_owner = functools.reduce(jnp.logical_or, [c == place for place in owners])
    not_owner = jnp.logical_not(is_owner)

    def push(source, target, sent, arrived, device):
        pltpu.make_async_remote_copy(
            src_ref=source,
            dst_ref=target,
            send_sem=sent,
            recv_sem=arrived,
            device_id=device,
            device_id_type=MESH,
        ).start()

    def wait_for(ref, sem):
        pltpu.make_async_copy(ref, ref, sem).wait()

    def user(o):
        return lax.rem(r + o, n_row), home

    def peer(o):
        return r, lax.rem(c + o, n_col)

    peers = far_first(n_col, y_count)
    users = far_first(n_col, n_col)

    loads = [
        pltpu.make_async_copy(source, target, load_sem.at[i])
        for i, (source, target) in enumerate(
            ((x_hbm, x_ref), (weight_hbm, weight_ref), (reach_hbm, reach_ref), (tile_hbm, tile_ref))
        )
    ]
    for load in loads:
        load.start()

    barrier = pltpu.get_barrier_semaphore()

    def greet(device):
        pl.semaphore_signal(barrier, inc=1, device_id=device, device_id_type=MESH)

    @pl.when(off_diagonal)
    def _():
        for o in range(n_col):
            greet((j, o))

    for o in peers:
        greet(peer(o))

    loads[0].wait()
    loads[1].wait()
    spread = rows_spread(x_ref[...])
    turned = jnp.transpose(jnp.concatenate([spread] * 4, axis=0))[0:16]
    weight = jnp.concatenate([weight_ref[...]] * 4, axis=1)
    scaled = jnp.where(iota((16, 128), 1) // 32 == iota((16, 128), 0) // 4, turned * weight, 0.0)
    eight = scaled[0:8] + scaled[8:16]
    piece = eight[0:4] + eight[4:8]
    z_ref[...] = piece
    slab_ref[0, c] = piece
    weight_row_ref[...] = weight

    pl.semaphore_wait(barrier, 2 * (n_col - 1))
    owner_flag = jnp.where(is_owner, 1, 0)
    for o in users:
        push(z_ref, slab_ref.at[1, c], z_sent.at[0], z_first_sem.at[owner_flag], user(o))
    for o in peers:
        push(z_ref, slab_ref.at[0, c], z_sent.at[0], z_row_sem.at[0], peer(o))

    group, slot = lax.div(c, 4), lax.rem(c, 4)
    keeper = owner(r, group)

    @pl.when(c == keeper)
    def _():
        weight_parts_ref[slot] = weight

    @pl.when(c != keeper)
    def _():
        push(weight_row_ref, weight_parts_ref.at[slot], weight_sent, weight_sem, (r, keeper))

    loads[2].wait()
    loads[3].wait()
    keep = jnp.where(d <= reach_ref[...], 1.0, 0.0) * jnp.where(r >= d, 1.0, 0.0)
    tile = tile_ref[...] * keep
    high_ref[0], low_ref[0] = split(tile)
    high_ref[1], low_ref[1] = split(jnp.transpose(tile))
    lone = jnp.where(off_diagonal, 0.0, 1.0)

    def multiply(sweep, near, far_vectors):
        mirror = dot_split(split(near), (high_ref[0], low_ref[0]), NN)
        for i in range(chunks):
            far_ref[sweep, i] = mirror[:, 128 * i : 128 * i + 128]

        @pl.when(off_diagonal)
        def _():
            if sweep == 0:
                wait_for(slab_ref.at[1, pl.ds(0, chunks)], z_first_sem.at[1])
            for turn in range(chunks):
                i = lax.rem(d + turn, chunks)
                push(
                    far_ref.at[sweep, i],
                    parts_ref.at[sweep, n_col - 2 + d],
                    far_sent.at[sweep],
                    part_sem.at[sweep],
                    (j, owner(j, i)),
                )

        forward = dot_split(split(far_vectors()), (high_ref[1], low_ref[1]), NN) + lone * mirror
        for i in range(chunks):
            own_ref[sweep, i] = forward[:, 128 * i : 128 * i + 128]
        for turn in range(chunks):
            i = lax.rem(c + turn, chunks)
            place = owner(r, i)

            @pl.when(c != place)
            def _():
                push(
                    own_ref.at[sweep, i],
                    parts_ref.at[sweep, lax.rem(place - c + n_col, n_col) - 1],
                    own_sent.at[sweep],
                    part_sem.at[sweep],
                    (r, place),
                )

    def total(sweep):
        wait_for(parts_ref.at[sweep], part_sem.at[sweep])
        return own_ref[sweep, mine] + jnp.sum(parts_ref[sweep], axis=0)

    side = jnp.where(off_diagonal, 1, 0)

    wait_for(slab_ref.at[0, pl.ds(0, n_col - 1)], z_row_sem.at[0])

    def far_pieces():
        @pl.when(off_diagonal)
        def _():
            wait_for(slab_ref.at[1, pl.ds(0, n_col - chunks)], z_first_sem.at[0])

        return slab_to_vectors(slab_ref[side])

    multiply(0, slab_to_vectors(slab_ref[0]), far_pieces)

    @pl.when(is_owner)
    def _():
        inside = mine == group

        @pl.when(inside)
        def _():
            wait_for(weight_parts_ref.at[pl.ds(0, 3)], weight_sem)

        @pl.when(jnp.logical_not(inside))
        def _():
            wait_for(weight_parts_ref, weight_sem)

        lane = iota((1, 128), 1) // SUB
        chunk_weight = sum(jnp.where(lane == i, weight_parts_ref[i], 0.0) for i in range(4))
        chunk_weight_ref[...] = chunk_weight
        values = total(0) * chunk_weight
        scaled = values * chunk_weight
        chunk_ref[...] = scaled
        wide_ref[0, mine] = scaled
        for o in peers:
            push(chunk_ref, wide_ref.at[0, mine], z_sent.at[1], z_row_sem.at[1], peer(o))
        for o in users:
            push(chunk_ref, wide_ref.at[1, mine], z_sent.at[1], z_col_sem, user(o))
        gram_first_ref[...] = gram_spread(values)
        if chunks > 1:
            wait_for(wide_ref.at[0, pl.ds(0, chunks - 1)], z_row_sem.at[1])

    @pl.when(not_owner)
    def _():
        wait_for(wide_ref.at[0], z_row_sem.at[1])

    def far_chunks():
        @pl.when(off_diagonal)
        def _():
            wait_for(wide_ref.at[1], z_col_sem)

        return jnp.concatenate([wide_ref[side, i] for i in range(chunks)], axis=1)

    multiply(1, jnp.concatenate([wide_ref[0, i] for i in range(chunks)], axis=1), far_chunks)

    @pl.when(is_owner)
    def _():
        values = total(1) * chunk_weight_ref[...]
        gram = rows_packed(gram_spread(values) + EPS * gram_first_ref[...])
        gram_ref[0] = gram
        gram_row_ref[mine] = gram
        for o in peers:
            push(gram_ref.at[0], gram_row_ref.at[mine], gram_sent.at[0], gram_sem.at[0], peer(o))
        turned = jnp.transpose(jnp.concatenate([values] * 8, axis=0))
        result_ref[...] = rows_packed(turned).reshape(4, 4, 128)
        for i in range(4):
            place = 4 * mine + i

            @pl.when(c == place)
            def _():
                back_ref[...] = result_ref[i]

            @pl.when(c != place)
            def _():
                push(result_ref.at[i], back_ref, back_sent, back_sem, (r, place))

        if chunks > 1:
            wait_for(gram_row_ref.at[pl.ds(0, chunks - 1)], gram_sem.at[0])

    @pl.when(not_owner)
    def _():
        wait_for(gram_row_ref, gram_sem.at[0])

    gram_own = jnp.sum(gram_row_ref[...], axis=0)
    gram_ref[1] = gram_own
    for o in far_first(n_row, n_col):
        row = lax.rem(r + o, n_row)
        push(gram_ref.at[1], gram_col_ref.at[o - 1], gram_sent.at[1], gram_sem.at[1], (row, c))

    @pl.when(c != keeper)
    def _():
        wait_for(back_ref, back_sem)

    back = split(jnp.concatenate([back_ref[...]] * 4, axis=0))
    wait_for(gram_col_ref, gram_sem.at[1])
    gram = rows_spread(gram_own + jnp.sum(gram_col_ref[...], axis=0))
    diagonal = jnp.where(iota((16, 128), 1) % K == iota((16, 128), 0), EPS * EPS, 0.0)
    solver = inverse_factor(gram * (1.0 / states) + diagonal)
    wide = jnp.concatenate([solver] * 8, axis=0)
    wide = jnp.where(iota((128, 128), 0) // K == iota((128, 128), 1) // K, wide, 0.0)
    out_ref[...] = dot_split(back, split(wide), NT)[0:4]

    wait_for(slab_ref.at[:, pl.ds(0, n_col - 1)], z_sent.at[0])
    wait_for(gram_col_ref, gram_sent.at[1])

    @pl.when(c != keeper)
    def _():
        wait_for(weight_row_ref, weight_sent)

    for sweep in range(2):

        @pl.when(off_diagonal)
        def _():
            wait_for(far_ref.at[sweep], far_sent.at[sweep])

        @pl.when(is_owner)
        def _():
            if chunks > 1:
                wait_for(own_ref.at[sweep, pl.ds(0, chunks - 1)], own_sent.at[sweep])

        @pl.when(not_owner)
        def _():
            wait_for(own_ref.at[sweep], own_sent.at[sweep])

    @pl.when(is_owner)
    def _():
        wait_for(parts_ref.at[0], z_sent.at[1])
        wait_for(gram_col_ref.at[pl.ds(0, n_col - 1)], gram_sent.at[0])

        @pl.when(mine == group)
        def _():
            wait_for(result_ref.at[pl.ds(0, 3)], back_sent)

        @pl.when(mine != group)
        def _():
            wait_for(result_ref, back_sent)


def local(start_modes, tiles, reach, weights, n_row, n_col):
    width = tiles.shape[-1]
    chunks = n_col // 4
    dma = pltpu.SemaphoreType.DMA
    out = pl.pallas_call(
        functools.partial(kernel, n_row, n_col, n_row * width),
        out_shape=pltpu.VMEM((4, 128), F32),
        in_specs=[pl.BlockSpec(memory_space=pltpu.HBM)] * 4,
        out_specs=pl.BlockSpec(memory_space=pltpu.VMEM),
        scratch_shapes=[
            pltpu.VMEM((4, 128), F32),
            pltpu.VMEM((width, width), F32),
            pltpu.VMEM((1, 1), jnp.int32),
            pltpu.VMEM((1, SUB), F32),
            pltpu.VMEM((2, width, width), BF16),
            pltpu.VMEM((2, width, width), BF16),
            pltpu.VMEM((1, 128), F32),
            pltpu.VMEM((4, 1, 128), F32),
            pltpu.VMEM((1, 128), F32),
            pltpu.VMEM((4, 128), F32),
            pltpu.VMEM((2, n_col, 4, 128), F32),
            pltpu.VMEM((2, chunks, K, 128), F32),
            pltpu.VMEM((2, chunks, K, 128), F32),
            pltpu.VMEM((2, 2 * (n_col - 1), K, 128), F32),
            pltpu.VMEM((K, 128), F32),
            pltpu.VMEM((2, chunks, K, 128), F32),
            pltpu.VMEM((K, 128), F32),
            pltpu.VMEM((2, 2, 128), F32),
            pltpu.VMEM((chunks, 2, 128), F32),
            pltpu.VMEM((n_row - 1, 2, 128), F32),
            pltpu.VMEM((4, 4, 128), F32),
            pltpu.VMEM((4, 128), F32),
            dma((4,)),
            dma(()),
            dma((2,)),
            dma((2,)),
            dma(()),
            dma((2,)),
            dma((2,)),
            dma(()),
            dma(()),
            dma((2,)),
            dma((2,)),
            dma((2,)),
            dma((2,)),
            dma(()),
        ],
        compiler_params=pltpu.CompilerParams(
            collective_id=0, has_side_effects=True, vmem_limit_bytes=60 * 1024 * 1024
        ),
    )(
        start_modes.reshape(4, 128),
        tiles.reshape(width, width),
        reach,
        weights.reshape(1, SUB),
    )
    return out.reshape(start_modes.shape)


def solution(mesh):
    return jax.shard_map(
        functools.partial(local, n_row=mesh.shape["trow"], n_col=mesh.shape["tcol"]),
        mesh=mesh,
        in_specs=(
            P(None, "trow", "tcol", None),
            P(None, "trow", "tcol", None, None, None),
            P(None, "trow"),
            P(None, "trow", "tcol", None),
        ),
        out_specs=P(None, "trow", "tcol", None),
        check_vma=False,
    )
```

```python
import functools

import jax
import jax.numpy as jnp
from jax import lax
from jax.experimental import pallas as pl
from jax.experimental.pallas import tpu as pltpu
from jax.sharding import PartitionSpec as P

K = 16
SUB = 32
EPS = 1e-06
F32 = jnp.float32
BF16 = jnp.bfloat16
MESH = pl.DeviceIdType.MESH
NT = (((1,), (1,)), ((), ()))
NN = (((1,), (0,)), ((), ()))


def iota(shape, axis):
    return lax.broadcasted_iota(jnp.int32, shape, axis)


def dot_half(a, b, dims):
    return lax.dot_general(a, b, dims, preferred_element_type=F32)


def swap_blocks(block):
    top, bottom = block[0:8], block[8:16]
    lane = iota((8, 128), 1)
    row = iota((8, 128), 0)
    low = lane < 64
    halves = (
        jnp.where(low, top, pltpu.roll(bottom, 64, 1)),
        jnp.where(low, pltpu.roll(top, 64, 1), bottom),
    )
    odd_lane = (lane // 32) % 2
    odd_row = row // 4
    done = []
    for half in halves:
        turned = pltpu.roll(half, 4, 0)
        moved = jnp.where(odd_lane == 1, pltpu.roll(turned, 32, 1), pltpu.roll(turned, 96, 1))
        done.append(jnp.where(odd_lane == odd_row, half, moved))
    return jnp.concatenate(done, axis=0)


def slab_to_vectors(slab):
    flat = slab.reshape(slab.shape[0] * 4, 128)
    return jnp.concatenate(
        [swap_blocks(flat[16 * i : 16 * i + 16]) for i in range(slab.shape[0] // 4)], axis=1
    )


def fold_lanes(value, shifts):
    for shift in shifts:
        value = value + pltpu.roll(value, shift, 1)
    return value


def rows_spread(packed):
    count = packed.shape[0]
    wide = jnp.concatenate(
        [jnp.broadcast_to(packed[a : a + 1], (8, 128)) for a in range(count)], axis=0
    )
    shape = (8 * count, 128)
    keep = iota(shape, 1) // 16 == iota(shape, 0) % 8
    return fold_lanes(jnp.where(keep, wide, 0.0), (64, 32, 16))


def rows_packed(spread):
    shape = spread.shape
    keep = iota(shape, 1) // 16 == iota(shape, 0) % 8
    held = jnp.where(keep, spread, 0.0)
    return jnp.concatenate(
        [jnp.sum(held[8 * a : 8 * a + 8], axis=0, keepdims=True) for a in range(shape[0] // 8)],
        axis=0,
    )


def split(value):
    high = value.astype(BF16)
    return high, (value - high.astype(F32)).astype(BF16)


def dot_split(a_parts, b_parts, dims):
    rows = a_parts[0].shape[0]
    both = dot_half(jnp.concatenate(a_parts, axis=0), b_parts[0], dims)
    return both[0:rows] + (both[rows:] + dot_half(a_parts[0], b_parts[1], dims))


def gram_spread(vectors):
    parts = split(vectors)
    return dot_split(parts, [jnp.concatenate([part] * 8, axis=0) for part in parts], NT)


def inverse_factor(gram):
    row = iota((8, 128), 0)
    tops = [jnp.broadcast_to(gram[0:8, k : k + 1], (8, 128)) for k in range(K)]
    bottoms = [jnp.broadcast_to(gram[8:16, k : k + 1], (8, 128)) for k in range(K)]
    unit = iota((8, 128), 1) % K
    right = [jnp.where(unit == row, 1.0, 0.0), jnp.where(unit == row + 8, 1.0, 0.0)]
    scale = [jnp.zeros((8, 128), F32), jnp.zeros((8, 128), F32)]
    for step in range(K):
        half, place = step // 8, step % 8
        here = (tops, bottoms)[half]
        pivot = here[step][place : place + 1]
        scale[half] = jnp.where(row == place, lax.rsqrt(pivot), scale[half])
        if step == K - 1:
            break
        inverse = 1.0 / pivot
        lines = [here[k][place : place + 1] for k in range(K)]
        right_line = right[half][place : place + 1]
        if step < 7:
            factor = jnp.where(row > place, tops[step] * inverse, 0.0)
            for k in range(step + 1, K):
                tops[k] = tops[k] - factor * lines[k]
            right[0] = right[0] - factor * right_line
        factor = bottoms[step] * inverse
        if half == 1:
            factor = jnp.where(row > place, factor, 0.0)
        for k in range(step + 1, K):
            bottoms[k] = bottoms[k] - factor * lines[k]
        right[1] = right[1] - factor * right_line
    return jnp.concatenate([right[0] * scale[0], right[1] * scale[1]], axis=0)


def far_first(count, period):
    return sorted(range(1, count), key=lambda o: (-min(o % period, period - o % period), o))


def kernel(
    n_row,
    n_col,
    states,
    x_hbm,
    tile_hbm,
    reach_hbm,
    weight_hbm,
    out_ref,
    x_ref,
    tile_ref,
    reach_ref,
    weight_ref,
    high_ref,
    low_ref,
    weight_row_ref,
    weight_parts_ref,
    chunk_weight_ref,
    z_ref,
    slab_ref,
    own_ref,
    far_ref,
    parts_ref,
    chunk_ref,
    wide_ref,
    gram_first_ref,
    gram_ref,
    gram_row_ref,
    gram_col_ref,
    result_ref,
    back_ref,
    load_sem,
    weight_sem,
    z_row_sem,
    z_first_sem,
    z_col_sem,
    part_sem,
    gram_sem,
    back_sem,
    weight_sent,
    z_sent,
    own_sent,
    far_sent,
    gram_sent,
    back_sent,
):
    r = lax.axis_index("trow")
    c = lax.axis_index("tcol")
    chunks = n_col // 4
    home = lax.rem(r, n_col)
    d = lax.rem(r - c + n_row, n_col)
    j = lax.rem(r - d + n_row, n_row)
    off_diagonal = d != 0
    y_count = n_col // 2

    def owner(row, chunk):
        place = lax.rem(row, n_col)
        x_low = lax.rem(lax.div(place, y_count) + lax.div(chunk, 2), 2)
        return x_low * y_count + lax.rem(place + y_count - 1 + 2 * lax.rem(chunk, 2), y_count)

    owners = [owner(r, i) for i in range(chunks)]
    mine = sum(jnp.where(c == place, i, 0) for i, place in enumerate(owners))
    is_owner = functools.reduce(jnp.logical_or, [c == place for place in owners])
    not_owner = jnp.logical_not(is_owner)

    def push(source, target, sent, arrived, device):
        pltpu.make_async_remote_copy(
            src_ref=source,
            dst_ref=target,
            send_sem=sent,
            recv_sem=arrived,
            device_id=device,
            device_id_type=MESH,
        ).start()

    def wait_for(ref, sem):
        pltpu.make_async_copy(ref, ref, sem).wait()

    def user(o):
        return lax.rem(r + o, n_row), home

    def peer(o):
        return r, lax.rem(c + o, n_col)

    peers = far_first(n_col, y_count)
    users = far_first(n_col, n_col)

    loads = [
        pltpu.make_async_copy(source, target, load_sem.at[i])
        for i, (source, target) in enumerate(
            ((x_hbm, x_ref), (weight_hbm, weight_ref), (reach_hbm, reach_ref), (tile_hbm, tile_ref))
        )
    ]
    for load in loads:
        load.start()

    barrier = pltpu.get_barrier_semaphore()

    def greet(device):
        pl.semaphore_signal(barrier, inc=1, device_id=device, device_id_type=MESH)

    @pl.when(off_diagonal)
    def _():
        for o in range(n_col):
            greet((j, o))

    for o in peers:
        greet(peer(o))

    loads[0].wait()
    loads[1].wait()
    spread = rows_spread(x_ref[...])
    turned = jnp.transpose(jnp.concatenate([spread] * 4, axis=0))[0:16]
    weight = jnp.concatenate([weight_ref[...]] * 4, axis=1)
    scaled = jnp.where(iota((16, 128), 1) // 32 == iota((16, 128), 0) // 4, turned * weight, 0.0)
    eight = scaled[0:8] + scaled[8:16]
    piece = eight[0:4] + eight[4:8]
    z_ref[...] = piece
    slab_ref[0, c] = piece
    weight_row_ref[...] = weight

    pl.semaphore_wait(barrier, 2 * (n_col - 1))
    owner_flag = jnp.where(is_owner, 1, 0)
    for o in users:
        push(z_ref, slab_ref.at[1, c], z_sent.at[0], z_first_sem.at[owner_flag], user(o))
    for o in peers:
        push(z_ref, slab_ref.at[0, c], z_sent.at[0], z_row_sem.at[0], peer(o))

    group, slot = lax.div(c, 4), lax.rem(c, 4)
    keeper = owner(r, group)

    @pl.when(c == keeper)
    def _():
        weight_parts_ref[slot] = weight

    @pl.when(c != keeper)
    def _():
        push(weight_row_ref, weight_parts_ref.at[slot], weight_sent, weight_sem, (r, keeper))

    loads[2].wait()
    loads[3].wait()
    keep = jnp.where(d <= reach_ref[...], 1.0, 0.0) * jnp.where(r >= d, 1.0, 0.0)
    tile = tile_ref[...] * keep
    high_ref[...], low_ref[...] = split(tile)
    lone = jnp.where(off_diagonal, 0.0, 1.0)

    def multiply(sweep, near, far_vectors):
        mirror = dot_split(split(near), (high_ref[...], low_ref[...]), NN)
        for i in range(chunks):
            far_ref[sweep, i] = mirror[:, 128 * i : 128 * i + 128]

        @pl.when(off_diagonal)
        def _():
            if sweep == 0:
                wait_for(slab_ref.at[1, pl.ds(0, chunks)], z_first_sem.at[1])
            for turn in range(chunks):
                i = lax.rem(d + turn, chunks)
                push(
                    far_ref.at[sweep, i],
                    parts_ref.at[sweep, n_col - 2 + d],
                    far_sent.at[sweep],
                    part_sem.at[sweep],
                    (j, owner(j, i)),
                )

        forward = dot_split(split(far_vectors()), (high_ref[...], low_ref[...]), NT) + lone * mirror
        for i in range(chunks):
            own_ref[sweep, i] = forward[:, 128 * i : 128 * i + 128]
        for turn in range(chunks):
            i = lax.rem(c + turn, chunks)
            place = owner(r, i)

            @pl.when(c != place)
            def _():
                push(
                    own_ref.at[sweep, i],
                    parts_ref.at[sweep, lax.rem(place - c + n_col, n_col) - 1],
                    own_sent.at[sweep],
                    part_sem.at[sweep],
                    (r, place),
                )

    def total(sweep):
        wait_for(parts_ref.at[sweep], part_sem.at[sweep])
        return own_ref[sweep, mine] + jnp.sum(parts_ref[sweep], axis=0)

    side = jnp.where(off_diagonal, 1, 0)

    wait_for(slab_ref.at[0, pl.ds(0, n_col - 1)], z_row_sem.at[0])

    def far_pieces():
        @pl.when(off_diagonal)
        def _():
            wait_for(slab_ref.at[1, pl.ds(0, n_col - chunks)], z_first_sem.at[0])

        return slab_to_vectors(slab_ref[side])

    multiply(0, slab_to_vectors(slab_ref[0]), far_pieces)

    @pl.when(is_owner)
    def _():
        inside = mine == group

        @pl.when(inside)
        def _():
            wait_for(weight_parts_ref.at[pl.ds(0, 3)], weight_sem)

        @pl.when(jnp.logical_not(inside))
        def _():
            wait_for(weight_parts_ref, weight_sem)

        lane = iota((1, 128), 1) // SUB
        chunk_weight = sum(jnp.where(lane == i, weight_parts_ref[i], 0.0) for i in range(4))
        chunk_weight_ref[...] = chunk_weight
        values = total(0) * chunk_weight
        scaled = values * chunk_weight
        chunk_ref[...] = scaled
        wide_ref[0, mine] = scaled
        for o in peers:
            push(chunk_ref, wide_ref.at[0, mine], z_sent.at[1], z_row_sem.at[1], peer(o))
        for o in users:
            push(chunk_ref, wide_ref.at[1, mine], z_sent.at[1], z_col_sem, user(o))
        gram_first_ref[...] = gram_spread(values)
        if chunks > 1:
            wait_for(wide_ref.at[0, pl.ds(0, chunks - 1)], z_row_sem.at[1])

    @pl.when(not_owner)
    def _():
        wait_for(wide_ref.at[0], z_row_sem.at[1])

    def far_chunks():
        @pl.when(off_diagonal)
        def _():
            wait_for(wide_ref.at[1], z_col_sem)

        return jnp.concatenate([wide_ref[side, i] for i in range(chunks)], axis=1)

    multiply(1, jnp.concatenate([wide_ref[0, i] for i in range(chunks)], axis=1), far_chunks)

    @pl.when(is_owner)
    def _():
        values = total(1) * chunk_weight_ref[...]
        gram = rows_packed(gram_spread(values) + EPS * gram_first_ref[...])
        gram_ref[0] = gram
        gram_row_ref[mine] = gram
        for o in peers:
            push(gram_ref.at[0], gram_row_ref.at[mine], gram_sent.at[0], gram_sem.at[0], peer(o))
        turned = jnp.transpose(jnp.concatenate([values] * 8, axis=0))
        result_ref[...] = rows_packed(turned).reshape(4, 4, 128)
        for i in range(4):
            place = 4 * mine + i

            @pl.when(c == place)
            def _():
                back_ref[...] = result_ref[i]

            @pl.when(c != place)
            def _():
                push(result_ref.at[i], back_ref, back_sent, back_sem, (r, place))

        if chunks > 1:
            wait_for(gram_row_ref.at[pl.ds(0, chunks - 1)], gram_sem.at[0])

    @pl.when(not_owner)
    def _():
        wait_for(gram_row_ref, gram_sem.at[0])

    gram_own = jnp.sum(gram_row_ref[...], axis=0)
    gram_ref[1] = gram_own
    for o in far_first(n_row, n_col):
        row = lax.rem(r + o, n_row)
        push(gram_ref.at[1], gram_col_ref.at[o - 1], gram_sent.at[1], gram_sem.at[1], (row, c))

    @pl.when(c != keeper)
    def _():
        wait_for(back_ref, back_sem)

    back = split(jnp.concatenate([back_ref[...]] * 4, axis=0))
    wait_for(gram_col_ref, gram_sem.at[1])
    gram = rows_spread(gram_own + jnp.sum(gram_col_ref[...], axis=0))
    diagonal = jnp.where(iota((16, 128), 1) % K == iota((16, 128), 0), EPS * EPS, 0.0)
    solver = inverse_factor(gram * (1.0 / states) + diagonal)
    wide = jnp.concatenate([solver] * 8, axis=0)
    wide = jnp.where(iota((128, 128), 0) // K == iota((128, 128), 1) // K, wide, 0.0)
    out_ref[...] = dot_split(back, split(wide), NT)[0:4]

    wait_for(slab_ref.at[:, pl.ds(0, n_col - 1)], z_sent.at[0])
    wait_for(gram_col_ref, gram_sent.at[1])

    @pl.when(c != keeper)
    def _():
        wait_for(weight_row_ref, weight_sent)

    for sweep in range(2):

        @pl.when(off_diagonal)
        def _():
            wait_for(far_ref.at[sweep], far_sent.at[sweep])

        @pl.when(is_owner)
        def _():
            if chunks > 1:
                wait_for(own_ref.at[sweep, pl.ds(0, chunks - 1)], own_sent.at[sweep])

        @pl.when(not_owner)
        def _():
            wait_for(own_ref.at[sweep], own_sent.at[sweep])

    @pl.when(is_owner)
    def _():
        wait_for(parts_ref.at[0], z_sent.at[1])
        wait_for(gram_col_ref.at[pl.ds(0, n_col - 1)], gram_sent.at[0])

        @pl.when(mine == group)
        def _():
            wait_for(result_ref.at[pl.ds(0, 3)], back_sent)

        @pl.when(mine != group)
        def _():
            wait_for(result_ref, back_sent)


def local(start_modes, tiles, reach, weights, n_row, n_col):
    width = tiles.shape[-1]
    chunks = n_col // 4
    dma = pltpu.SemaphoreType.DMA
    out = pl.pallas_call(
        functools.partial(kernel, n_row, n_col, n_row * width),
        out_shape=pltpu.VMEM((4, 128), F32),
        in_specs=[pl.BlockSpec(memory_space=pltpu.HBM)] * 4,
        out_specs=pl.BlockSpec(memory_space=pltpu.VMEM),
        scratch_shapes=[
            pltpu.VMEM((4, 128), F32),
            pltpu.VMEM((width, width), F32),
            pltpu.VMEM((1, 1), jnp.int32),
            pltpu.VMEM((1, SUB), F32),
            pltpu.VMEM((width, width), BF16),
            pltpu.VMEM((width, width), BF16),
            pltpu.VMEM((1, 128), F32),
            pltpu.VMEM((4, 1, 128), F32),
            pltpu.VMEM((1, 128), F32),
            pltpu.VMEM((4, 128), F32),
            pltpu.VMEM((2, n_col, 4, 128), F32),
            pltpu.VMEM((2, chunks, K, 128), F32),
            pltpu.VMEM((2, chunks, K, 128), F32),
            pltpu.VMEM((2, 2 * (n_col - 1), K, 128), F32),
            pltpu.VMEM((K, 128), F32),
            pltpu.VMEM((2, chunks, K, 128), F32),
            pltpu.VMEM((K, 128), F32),
            pltpu.VMEM((2, 2, 128), F32),
            pltpu.VMEM((chunks, 2, 128), F32),
            pltpu.VMEM((n_row - 1, 2, 128), F32),
            pltpu.VMEM((4, 4, 128), F32),
            pltpu.VMEM((4, 128), F32),
            dma((4,)),
            dma(()),
            dma((2,)),
            dma((2,)),
            dma(()),
            dma((2,)),
            dma((2,)),
            dma(()),
            dma(()),
            dma((2,)),
            dma((2,)),
            dma((2,)),
            dma((2,)),
            dma(()),
        ],
        compiler_params=pltpu.CompilerParams(
            collective_id=0, has_side_effects=True, vmem_limit_bytes=60 * 1024 * 1024
        ),
    )(
        start_modes.reshape(4, 128),
        tiles.reshape(width, width),
        reach,
        weights.reshape(1, SUB),
    )
    return out.reshape(start_modes.shape)


def solution(mesh):
    return jax.shard_map(
        functools.partial(local, n_row=mesh.shape["trow"], n_col=mesh.shape["tcol"]),
        mesh=mesh,
        in_specs=(
            P(None, "trow", "tcol", None),
            P(None, "trow", "tcol", None, None, None),
            P(None, "trow"),
            P(None, "trow", "tcol", None),
        ),
        out_specs=P(None, "trow", "tcol", None),
        check_vma=False,
    )
```

```python
import functools

import jax
import jax.numpy as jnp
from jax import lax
from jax.experimental import pallas as pl
from jax.experimental.pallas import tpu as pltpu
from jax.sharding import PartitionSpec as P

K = 16
SUB = 32
EPS = 1e-06
F32 = jnp.float32
BF16 = jnp.bfloat16
MESH = pl.DeviceIdType.MESH
NT = (((1,), (1,)), ((), ()))
NN = (((1,), (0,)), ((), ()))


def iota(shape, axis):
    return lax.broadcasted_iota(jnp.int32, shape, axis)


def dot_half(a, b, dims):
    return lax.dot_general(a, b, dims, preferred_element_type=F32)


def swap_blocks(block):
    top, bottom = block[0:8], block[8:16]
    lane = iota((8, 128), 1)
    row = iota((8, 128), 0)
    low = lane < 64
    halves = (
        jnp.where(low, top, pltpu.roll(bottom, 64, 1)),
        jnp.where(low, pltpu.roll(top, 64, 1), bottom),
    )
    odd_lane = (lane // 32) % 2
    odd_row = row // 4
    done = []
    for half in halves:
        turned = pltpu.roll(half, 4, 0)
        moved = jnp.where(odd_lane == 1, pltpu.roll(turned, 32, 1), pltpu.roll(turned, 96, 1))
        done.append(jnp.where(odd_lane == odd_row, half, moved))
    return jnp.concatenate(done, axis=0)


def slab_to_vectors(slab):
    flat = slab.reshape(slab.shape[0] * 4, 128)
    return jnp.concatenate(
        [swap_blocks(flat[16 * i : 16 * i + 16]) for i in range(slab.shape[0] // 4)], axis=1
    )


def fold_lanes(value, shifts):
    for shift in shifts:
        value = value + pltpu.roll(value, shift, 1)
    return value


def rows_spread(packed):
    count = packed.shape[0]
    wide = jnp.concatenate(
        [jnp.broadcast_to(packed[a : a + 1], (8, 128)) for a in range(count)], axis=0
    )
    shape = (8 * count, 128)
    keep = iota(shape, 1) // 16 == iota(shape, 0) % 8
    return fold_lanes(jnp.where(keep, wide, 0.0), (64, 32, 16))


def rows_packed(spread, backward=False):
    shape = spread.shape
    place = iota(shape, 0) % 8
    keep = iota(shape, 1) // 16 == (7 - place if backward else place)
    held = jnp.where(keep, spread, 0.0)
    return jnp.concatenate(
        [jnp.sum(held[8 * a : 8 * a + 8], axis=0, keepdims=True) for a in range(shape[0] // 8)],
        axis=0,
    )


def split(value):
    high = value.astype(BF16)
    return high, (value - high.astype(F32)).astype(BF16)


def dot_split(a_parts, b_parts, dims):
    rows = a_parts[0].shape[0]
    both = dot_half(jnp.concatenate(a_parts, axis=0), b_parts[0], dims)
    return both[0:rows] + (both[rows:] + dot_half(a_parts[0], b_parts[1], dims))


def gram_spread(vectors):
    parts = split(vectors)
    return dot_split(parts, [jnp.concatenate([part] * 8, axis=0) for part in parts], NT)


def inverse_factor(gram):
    row = iota((8, 128), 0)
    columns = [
        [jnp.broadcast_to(gram[8 * half : 8 * half + 8, k : k + 1], (8, 128)) for k in range(K)]
        for half in range(2)
    ]
    unit = iota((8, 128), 1) % K
    right = [jnp.where(unit == row + 8 * half, 1.0, 0.0) for half in range(2)]
    done = []
    for step in range(0, K, 2):
        half, place = step // 8, step % 8
        here = columns[half]
        first = [here[k][place : place + 1] for k in range(K)]
        second = [here[k][place + 1 : place + 2] for k in range(K)]
        right_first = right[half][place : place + 1]
        right_second = right[half][place + 1 : place + 2]
        top, side, last = first[step], second[step], second[step + 1]
        ratio = side / top
        done.append(right_first * lax.rsqrt(top))
        done.append((right_second - ratio * right_first) * lax.rsqrt(last - ratio * side))
        if step == K - 2:
            break
        inverse = 1.0 / (top * last - side * side)
        for part in range(half, 2):
            one, two = columns[part][step], columns[part][step + 1]
            factor_one = (last * one - side * two) * inverse
            factor_two = (top * two - side * one) * inverse
            if part == half:
                below = row > place + 1
                factor_one = jnp.where(below, factor_one, 0.0)
                factor_two = jnp.where(below, factor_two, 0.0)
            for k in range(step + 2, K):
                columns[part][k] = columns[part][k] - (factor_one * first[k] + factor_two * second[k])
            right[part] = right[part] - (factor_one * right_first + factor_two * right_second)
    return jnp.concatenate(done, axis=0)


def far_first(count, period):
    return sorted(range(1, count), key=lambda o: (-min(o % period, period - o % period), o))


def kernel(
    n_row,
    n_col,
    states,
    x_hbm,
    tile_hbm,
    reach_hbm,
    weight_hbm,
    out_ref,
    x_ref,
    tile_ref,
    reach_ref,
    weight_ref,
    high_ref,
    low_ref,
    weight_row_ref,
    weight_parts_ref,
    chunk_weight_ref,
    z_ref,
    slab_ref,
    own_ref,
    far_ref,
    parts_ref,
    chunk_ref,
    wide_ref,
    gram_first_ref,
    gram_ref,
    gram_row_ref,
    gram_col_ref,
    result_ref,
    back_ref,
    load_sem,
    weight_sem,
    z_row_sem,
    z_near_sem,
    z_first_sem,
    z_col_sem,
    part_sem,
    gram_sem,
    back_sem,
    weight_sent,
    z_sent,
    own_sent,
    far_sent,
    gram_sent,
    back_sent,
):
    r = lax.axis_index("trow")
    c = lax.axis_index("tcol")
    chunks = n_col // 4
    home = lax.rem(r, n_col)
    d = lax.rem(r - c + n_row, n_col)
    j = lax.rem(r - d + n_row, n_row)
    off_diagonal = d != 0
    y_count = n_col // 2
    per_half = min(2, chunks)
    halves = chunks // per_half
    span = 128 * per_half

    def owner(row, chunk):
        place = lax.rem(row, n_col)
        x_low = lax.rem(lax.div(place, y_count) + lax.div(chunk, 2), 2)
        return x_low * y_count + lax.rem(place + y_count - 1 + 2 * lax.rem(chunk, 2), y_count)

    owners = [owner(r, i) for i in range(chunks)]
    size = chunks // 2
    mine = sum(jnp.where(c == place, i, 0) for i, place in enumerate(owners))
    is_owner = functools.reduce(jnp.logical_or, [c == place for place in owners])
    not_owner = jnp.logical_not(is_owner)

    def push(source, target, sent, arrived, device):
        pltpu.make_async_remote_copy(
            src_ref=source,
            dst_ref=target,
            send_sem=sent,
            recv_sem=arrived,
            device_id=device,
            device_id_type=MESH,
        ).start()

    def wait_for(ref, sem):
        pltpu.make_async_copy(ref, ref, sem).wait()

    def user(o):
        return lax.rem(r + o, n_row), home

    def peer(o):
        return r, lax.rem(c + o, n_col)

    peers = far_first(n_col, y_count)
    users = far_first(n_col, n_col)

    loads = [
        pltpu.make_async_copy(source, target, load_sem.at[i])
        for i, (source, target) in enumerate(
            ((x_hbm, x_ref), (weight_hbm, weight_ref), (reach_hbm, reach_ref), (tile_hbm, tile_ref))
        )
    ]
    for load in loads:
        load.start()

    barrier = pltpu.get_barrier_semaphore()

    def greet(device):
        pl.semaphore_signal(barrier, inc=1, device_id=device, device_id_type=MESH)

    @pl.when(off_diagonal)
    def _():
        for o in range(n_col):
            greet((j, o))

    for o in peers:
        greet(peer(o))

    loads[0].wait()
    loads[1].wait()
    spread = rows_spread(x_ref[...])
    turned = jnp.transpose(jnp.concatenate([spread] * 4, axis=0))[0:16]
    weight = jnp.concatenate([weight_ref[...]] * 4, axis=1)
    scaled = jnp.where(iota((16, 128), 1) // 32 == iota((16, 128), 0) // 4, turned * weight, 0.0)
    eight = scaled[0:8] + scaled[8:16]
    piece = eight[0:4] + eight[4:8]
    z_ref[...] = piece
    slab_ref[0, c] = piece
    weight_row_ref[...] = weight

    pl.semaphore_wait(barrier, 2 * (n_col - 1))
    owner_flag = jnp.where(is_owner, 1, 0)
    for o in users:
        push(z_ref, slab_ref.at[1, c], z_sent.at[0], z_first_sem.at[owner_flag], user(o))
    for o in peers:
        push(z_ref, slab_ref.at[0, c], z_sent.at[0], z_row_sem, peer(o))

    group, slot = lax.div(c, 4), lax.rem(c, 4)
    keeper = owner(r, group)

    @pl.when(c == keeper)
    def _():
        weight_parts_ref[slot] = weight

    @pl.when(c != keeper)
    def _():
        push(weight_row_ref, weight_parts_ref.at[slot], weight_sent, weight_sem, (r, keeper))

    loads[3].wait()
    tile = tile_ref[...]
    high_ref[0], low_ref[0] = split(tile)
    high_ref[1], low_ref[1] = split(jnp.transpose(tile))
    loads[2].wait()
    keep = jnp.where(d <= reach_ref[...], 1.0, 0.0) * jnp.where(r >= d, 1.0, 0.0)
    lone = jnp.where(off_diagonal, 0.0, 1.0)

    def multiply(sweep, mirror_half, far_vectors):
        mirror = []
        for part in range(halves):
            lanes = slice(part * span, part * span + span)
            mirror.append(mirror_half(lanes))
            for i in range(per_half):
                far_ref[sweep, part * per_half + i] = mirror[part][:, 128 * i : 128 * i + 128]

            @pl.when(off_diagonal)
            def _():
                if sweep == 0 and part == 0:
                    wait_for(slab_ref.at[1, pl.ds(0, chunks)], z_first_sem.at[1])
                for turn in range(per_half):
                    i = part * per_half + lax.rem(d + turn, per_half)
                    push(
                        far_ref.at[sweep, i],
                        parts_ref.at[sweep, n_col - 2 + d],
                        far_sent.at[sweep],
                        part_sem.at[sweep],
                        (j, owner(j, i)),
                    )

        pieces = split(far_vectors() * keep)
        for part in range(halves):
            lanes = slice(part * span, part * span + span)
            forward = dot_split(pieces, (high_ref[1, :, lanes], low_ref[1, :, lanes]), NN)
            forward = forward + lone * mirror[part]
            for i in range(per_half):
                own_ref[sweep, part * per_half + i] = forward[:, 128 * i : 128 * i + 128]
            for turn in range(per_half):
                i = part * per_half + lax.rem(c + turn, per_half)
                place = owner(r, i)

                @pl.when(c != place)
                def _():
                    push(
                        own_ref.at[sweep, i],
                        parts_ref.at[sweep, lax.rem(place - c + n_col, n_col) - 1],
                        own_sent.at[sweep],
                        part_sem.at[sweep],
                        (r, place),
                    )

    def total(sweep):
        wait_for(parts_ref.at[sweep], part_sem.at[sweep])
        return own_ref[sweep, mine] + jnp.sum(parts_ref[sweep], axis=0)

    side = jnp.where(off_diagonal, 1, 0)

    wait_for(slab_ref.at[0, pl.ds(0, n_col - 1)], z_row_sem)

    def far_pieces():
        @pl.when(off_diagonal)
        def _():
            wait_for(slab_ref.at[1, pl.ds(0, n_col - chunks)], z_first_sem.at[0])

        return slab_to_vectors(slab_ref[side])

    near = split(slab_to_vectors(slab_ref[0]) * keep)

    def first_half(lanes):
        return dot_split(near, (high_ref[0, :, lanes], low_ref[0, :, lanes]), NN)

    multiply(0, first_half, far_pieces)

    @pl.when(is_owner)
    def _():
        inside = mine == group

        @pl.when(inside)
        def _():
            wait_for(weight_parts_ref.at[pl.ds(0, 3)], weight_sem)

        @pl.when(jnp.logical_not(inside))
        def _():
            wait_for(weight_parts_ref, weight_sem)

        lane = iota((1, 128), 1) // SUB
        chunk_weight = sum(jnp.where(lane == i, weight_parts_ref[i], 0.0) for i in range(4))
        chunk_weight_ref[...] = chunk_weight
        values = total(0) * chunk_weight
        scaled = values * chunk_weight
        chunk_ref[...] = scaled
        wide_ref[0, mine] = scaled
        for o in peers:
            push(chunk_ref, wide_ref.at[0, mine], z_sent.at[1], z_near_sem.at[lax.div(mine, size)], peer(o))
        for o in users:
            push(chunk_ref, wide_ref.at[1, mine], z_sent.at[1], z_col_sem, user(o))
        gram_first_ref[...] = gram_spread(values)

    def near_part(part):
        own_part = jnp.logical_and(is_owner, lax.div(mine, size) == part)

        @pl.when(own_part)
        def _():
            if size > 1:
                wait_for(wide_ref.at[0, pl.ds(0, size - 1)], z_near_sem.at[part])

        @pl.when(jnp.logical_not(own_part))
        def _():
            wait_for(wide_ref.at[0, pl.ds(0, size)], z_near_sem.at[part])

        vectors = split(jnp.concatenate([wide_ref[0, size * part + i] for i in range(size)], axis=1) * keep)
        rows = pl.ds(pl.multiple_of(part * (128 * size), 128 * size), 128 * size)
        return lambda lanes: dot_split(vectors, (high_ref[0, rows, lanes], low_ref[0, rows, lanes]), NN)

    nearer = jnp.where(lax.div(c, y_count) == lax.div(home, y_count), 0, 1)
    product = near_part(nearer)
    early = [product(slice(part * span, part * span + span)) for part in range(halves)]
    product = near_part(1 - nearer)

    def second_half(lanes):
        return early[lanes.start // span] + product(lanes)

    def far_chunks():
        @pl.when(off_diagonal)
        def _():
            wait_for(wide_ref.at[1], z_col_sem)

        return jnp.concatenate([wide_ref[side, i] for i in range(chunks)], axis=1)

    multiply(1, second_half, far_chunks)

    @pl.when(is_owner)
    def _():
        values = total(1) * chunk_weight_ref[...]
        gram = rows_packed(gram_spread(values) + EPS * gram_first_ref[...], backward=True)
        gram_ref[0] = gram
        gram_row_ref[mine] = gram
        for o in peers:
            push(gram_ref.at[0], gram_row_ref.at[mine], gram_sent.at[0], gram_sem.at[0], peer(o))
        turned = jnp.transpose(jnp.concatenate([values] * 8, axis=0))
        result_ref[...] = rows_packed(turned).reshape(4, 4, 128)
        for i in range(4):
            place = 4 * mine + i

            @pl.when(c == place)
            def _():
                back_ref[...] = result_ref[i]

            @pl.when(c != place)
            def _():
                push(result_ref.at[i], back_ref, back_sent, back_sem, (r, place))

        if chunks > 1:
            wait_for(gram_row_ref.at[pl.ds(0, chunks - 1)], gram_sem.at[0])

    @pl.when(not_owner)
    def _():
        wait_for(gram_row_ref, gram_sem.at[0])

    gram_own = jnp.sum(gram_row_ref[...], axis=0)
    gram_ref[1] = gram_own
    for o in far_first(n_row, n_col):
        row = lax.rem(r + o, n_row)
        push(gram_ref.at[1], gram_col_ref.at[o - 1], gram_sent.at[1], gram_sem.at[1], (row, c))

    @pl.when(c != keeper)
    def _():
        wait_for(back_ref, back_sem)

    back = split(jnp.concatenate([back_ref[...]] * 4, axis=0))
    wait_for(gram_col_ref, gram_sem.at[1])
    total_gram = gram_own + jnp.sum(gram_col_ref[...], axis=0)
    gram = jnp.concatenate(
        [
            pltpu.roll(jnp.broadcast_to(total_gram[i : i + 1], (8, 128)), K, 1, stride=K, stride_axis=0)
            for i in range(2)
        ],
        axis=0,
    )
    diagonal = jnp.where(iota((16, 128), 1) == iota((16, 128), 0), EPS * EPS, 0.0)
    solver = inverse_factor(gram * (1.0 / states) + diagonal)
    wide = jnp.concatenate([solver] * 8, axis=0)
    wide = jnp.where(iota((128, 128), 0) // K == iota((128, 128), 1) // K, wide, 0.0)
    out_ref[...] = dot_split(back, split(wide), NT)[0:4]

    wait_for(slab_ref.at[:, pl.ds(0, n_col - 1)], z_sent.at[0])
    wait_for(gram_col_ref, gram_sent.at[1])

    @pl.when(c != keeper)
    def _():
        wait_for(weight_row_ref, weight_sent)

    for sweep in range(2):

        @pl.when(off_diagonal)
        def _():
            wait_for(far_ref.at[sweep], far_sent.at[sweep])

        @pl.when(is_owner)
        def _():
            if chunks > 1:
                wait_for(own_ref.at[sweep, pl.ds(0, chunks - 1)], own_sent.at[sweep])

        @pl.when(not_owner)
        def _():
            wait_for(own_ref.at[sweep], own_sent.at[sweep])

    @pl.when(is_owner)
    def _():
        wait_for(parts_ref.at[0], z_sent.at[1])
        wait_for(gram_col_ref.at[pl.ds(0, n_col - 1)], gram_sent.at[0])

        @pl.when(mine == group)
        def _():
            wait_for(result_ref.at[pl.ds(0, 3)], back_sent)

        @pl.when(mine != group)
        def _():
            wait_for(result_ref, back_sent)


def local(start_modes, tiles, reach, weights, n_row, n_col):
    width = tiles.shape[-1]
    chunks = n_col // 4
    dma = pltpu.SemaphoreType.DMA
    out = pl.pallas_call(
        functools.partial(kernel, n_row, n_col, n_row * width),
        out_shape=pltpu.VMEM((4, 128), F32),
        in_specs=[pl.BlockSpec(memory_space=pltpu.HBM)] * 4,
        out_specs=pl.BlockSpec(memory_space=pltpu.VMEM),
        scratch_shapes=[
            pltpu.VMEM((4, 128), F32),
            pltpu.VMEM((width, width), F32),
            pltpu.VMEM((1, 1), jnp.int32),
            pltpu.VMEM((1, SUB), F32),
            pltpu.VMEM((2, width, width), BF16),
            pltpu.VMEM((2, width, width), BF16),
            pltpu.VMEM((1, 128), F32),
            pltpu.VMEM((4, 1, 128), F32),
            pltpu.VMEM((1, 128), F32),
            pltpu.VMEM((4, 128), F32),
            pltpu.VMEM((2, n_col, 4, 128), F32),
            pltpu.VMEM((2, chunks, K, 128), F32),
            pltpu.VMEM((2, chunks, K, 128), F32),
            pltpu.VMEM((2, 2 * (n_col - 1), K, 128), F32),
            pltpu.VMEM((K, 128), F32),
            pltpu.VMEM((2, chunks, K, 128), F32),
            pltpu.VMEM((K, 128), F32),
            pltpu.VMEM((2, 2, 128), F32),
            pltpu.VMEM((chunks, 2, 128), F32),
            pltpu.VMEM((n_row - 1, 2, 128), F32),
            pltpu.VMEM((4, 4, 128), F32),
            pltpu.VMEM((4, 128), F32),
            dma((4,)),
            dma(()),
            dma(()),
            dma((2,)),
            dma((2,)),
            dma(()),
            dma((2,)),
            dma((2,)),
            dma(()),
            dma(()),
            dma((2,)),
            dma((2,)),
            dma((2,)),
            dma((2,)),
            dma(()),
        ],
        compiler_params=pltpu.CompilerParams(
            collective_id=0, has_side_effects=True, vmem_limit_bytes=60 * 1024 * 1024
        ),
    )(
        start_modes.reshape(4, 128),
        tiles.reshape(width, width),
        reach,
        weights.reshape(1, SUB),
    )
    return out.reshape(start_modes.shape)


def solution(mesh):
    return jax.shard_map(
        functools.partial(local, n_row=mesh.shape["trow"], n_col=mesh.shape["tcol"]),
        mesh=mesh,
        in_specs=(
            P(None, "trow", "tcol", None),
            P(None, "trow", "tcol", None, None, None),
            P(None, "trow"),
            P(None, "trow", "tcol", None),
        ),
        out_specs=P(None, "trow", "tcol", None),
        check_vma=False,
    )
```

```python
import functools

import jax
import jax.numpy as jnp
from jax import lax
from jax.experimental import pallas as pl
from jax.experimental.pallas import tpu as pltpu
from jax.sharding import PartitionSpec as P

K = 16
SUB = 32
EPS = 1e-06
F32 = jnp.float32
BF16 = jnp.bfloat16
MESH = pl.DeviceIdType.MESH
NT = (((1,), (1,)), ((), ()))
NN = (((1,), (0,)), ((), ()))


def iota(shape, axis):
    return lax.broadcasted_iota(jnp.int32, shape, axis)


def dot_half(a, b, dims):
    return lax.dot_general(a, b, dims, preferred_element_type=F32)


def swap_blocks(block):
    top, bottom = block[0:8], block[8:16]
    lane = iota((8, 128), 1)
    row = iota((8, 128), 0)
    low = lane < 64
    halves = (
        jnp.where(low, top, pltpu.roll(bottom, 64, 1)),
        jnp.where(low, pltpu.roll(top, 64, 1), bottom),
    )
    odd_lane = (lane // 32) % 2
    odd_row = row // 4
    done = []
    for half in halves:
        turned = pltpu.roll(half, 4, 0)
        moved = jnp.where(odd_lane == 1, pltpu.roll(turned, 32, 1), pltpu.roll(turned, 96, 1))
        done.append(jnp.where(odd_lane == odd_row, half, moved))
    return jnp.concatenate(done, axis=0)


def slab_to_vectors(slab):
    flat = slab.reshape(slab.shape[0] * 4, 128)
    return jnp.concatenate(
        [swap_blocks(flat[16 * i : 16 * i + 16]) for i in range(slab.shape[0] // 4)], axis=1
    )


def fold_lanes(value, shifts):
    for shift in shifts:
        value = value + pltpu.roll(value, shift, 1)
    return value


def rows_spread(packed):
    count = packed.shape[0]
    wide = jnp.concatenate(
        [jnp.broadcast_to(packed[a : a + 1], (8, 128)) for a in range(count)], axis=0
    )
    shape = (8 * count, 128)
    keep = iota(shape, 1) // 16 == iota(shape, 0) % 8
    return fold_lanes(jnp.where(keep, wide, 0.0), (64, 32, 16))


def rows_packed(spread, backward=False):
    shape = spread.shape
    place = iota(shape, 0) % 8
    keep = iota(shape, 1) // 16 == (7 - place if backward else place)
    held = jnp.where(keep, spread, 0.0)
    return jnp.concatenate(
        [jnp.sum(held[8 * a : 8 * a + 8], axis=0, keepdims=True) for a in range(shape[0] // 8)],
        axis=0,
    )


def split(value):
    high = value.astype(BF16)
    return high, (value - high.astype(F32)).astype(BF16)


def dot_split(a_parts, b_parts, dims):
    rows = a_parts[0].shape[0]
    both = dot_half(jnp.concatenate(a_parts, axis=0), b_parts[0], dims)
    return both[0:rows] + (both[rows:] + dot_half(a_parts[0], b_parts[1], dims))


def gram_spread(vectors):
    parts = split(vectors)
    return dot_split(parts, [jnp.concatenate([part] * 8, axis=0) for part in parts], NT)


def inverse_factor(gram):
    row = iota((8, 128), 0)
    columns = [
        [jnp.broadcast_to(gram[8 * half : 8 * half + 8, k : k + 1], (8, 128)) for k in range(K)]
        for half in range(2)
    ]
    unit = iota((8, 128), 1) % K
    right = [jnp.where(unit == row + 8 * half, 1.0, 0.0) for half in range(2)]
    done = []
    for step in range(0, K, 2):
        half, place = step // 8, step % 8
        here = columns[half]
        first = [here[k][place : place + 1] for k in range(K)]
        second = [here[k][place + 1 : place + 2] for k in range(K)]
        right_first = right[half][place : place + 1]
        right_second = right[half][place + 1 : place + 2]
        top, side, last = first[step], second[step], second[step + 1]
        ratio = side / top
        done.append(right_first * lax.rsqrt(top))
        done.append((right_second - ratio * right_first) * lax.rsqrt(last - ratio * side))
        if step == K - 2:
            break
        inverse = 1.0 / (top * last - side * side)
        for part in range(half, 2):
            one, two = columns[part][step], columns[part][step + 1]
            factor_one = (last * one - side * two) * inverse
            factor_two = (top * two - side * one) * inverse
            if part == half:
                below = row > place + 1
                factor_one = jnp.where(below, factor_one, 0.0)
                factor_two = jnp.where(below, factor_two, 0.0)
            for k in range(step + 2, K):
                columns[part][k] = columns[part][k] - (factor_one * first[k] + factor_two * second[k])
            right[part] = right[part] - (factor_one * right_first + factor_two * right_second)
    return jnp.concatenate(done, axis=0)


def far_first(count, period):
    return sorted(range(1, count), key=lambda o: (-min(o % period, period - o % period), o))


def kernel(
    n_row,
    n_col,
    states,
    x_hbm,
    tile_hbm,
    reach_hbm,
    weight_hbm,
    out_ref,
    x_ref,
    tile_ref,
    reach_ref,
    weight_ref,
    high_ref,
    low_ref,
    weight_row_ref,
    weight_parts_ref,
    chunk_weight_ref,
    z_ref,
    slab_ref,
    own_ref,
    far_ref,
    parts_ref,
    chunk_ref,
    wide_ref,
    gram_first_ref,
    gram_ref,
    gram_row_ref,
    gram_col_ref,
    result_ref,
    back_ref,
    load_sem,
    weight_sem,
    z_row_sem,
    z_near_sem,
    z_first_sem,
    z_col_sem,
    part_sem,
    gram_sem,
    back_sem,
    weight_sent,
    z_sent,
    own_sent,
    far_sent,
    gram_sent,
    back_sent,
):
    r = lax.axis_index("trow")
    c = lax.axis_index("tcol")
    chunks = n_col // 4
    home = lax.rem(r, n_col)
    d = lax.rem(r - c + n_row, n_col)
    j = lax.rem(r - d + n_row, n_row)
    off_diagonal = d != 0
    y_count = n_col // 2
    per_half = min(2, chunks)
    halves = chunks // per_half
    span = 128 * per_half

    def owner(row, chunk):
        place = lax.rem(row, n_col)
        x_low = lax.rem(lax.div(place, y_count) + lax.div(chunk, 2), 2)
        return x_low * y_count + lax.rem(place + y_count - 1 + 2 * lax.rem(chunk, 2), y_count)

    owners = [owner(r, i) for i in range(chunks)]
    size = chunks // 2
    mine = sum(jnp.where(c == place, i, 0) for i, place in enumerate(owners))
    is_owner = functools.reduce(jnp.logical_or, [c == place for place in owners])
    not_owner = jnp.logical_not(is_owner)

    def push(source, target, sent, arrived, device):
        pltpu.make_async_remote_copy(
            src_ref=source,
            dst_ref=target,
            send_sem=sent,
            recv_sem=arrived,
            device_id=device,
            device_id_type=MESH,
        ).start()

    def wait_for(ref, sem):
        pltpu.make_async_copy(ref, ref, sem).wait()

    def user(o):
        return lax.rem(r + o, n_row), home

    def peer(o):
        return r, lax.rem(c + o, n_col)

    peers = far_first(n_col, y_count)
    users = far_first(n_col, n_col)

    loads = [
        pltpu.make_async_copy(source, target, load_sem.at[i])
        for i, (source, target) in enumerate(
            ((x_hbm, x_ref), (weight_hbm, weight_ref), (reach_hbm, reach_ref), (tile_hbm, tile_ref))
        )
    ]
    barrier = pltpu.get_barrier_semaphore()

    def greet(device):
        pl.semaphore_signal(barrier, inc=1, device_id=device, device_id_type=MESH)

    @pl.when(off_diagonal)
    def _():
        for o in range(n_col):
            greet((j, o))

    for o in peers:
        greet(peer(o))
    for load in loads:
        load.start()

    loads[0].wait()
    loads[1].wait()
    spread = rows_spread(x_ref[...])
    turned = jnp.transpose(jnp.concatenate([spread] * 4, axis=0))[0:16]
    weight = jnp.concatenate([weight_ref[...]] * 4, axis=1)
    scaled = jnp.where(iota((16, 128), 1) // 32 == iota((16, 128), 0) // 4, turned * weight, 0.0)
    eight = scaled[0:8] + scaled[8:16]
    piece = eight[0:4] + eight[4:8]
    z_ref[...] = piece
    slab_ref[0, c] = piece
    weight_row_ref[...] = weight

    pl.semaphore_wait(barrier, 2 * (n_col - 1))
    owner_flag = jnp.where(is_owner, 1, 0)
    for o in users:
        push(z_ref, slab_ref.at[1, c], z_sent.at[0], z_first_sem.at[owner_flag], user(o))
    for o in peers:
        push(z_ref, slab_ref.at[0, c], z_sent.at[0], z_row_sem, peer(o))

    group, slot = lax.div(c, 4), lax.rem(c, 4)
    keeper = owner(r, group)

    @pl.when(c == keeper)
    def _():
        weight_parts_ref[slot] = weight

    @pl.when(c != keeper)
    def _():
        push(weight_row_ref, weight_parts_ref.at[slot], weight_sent, weight_sem, (r, keeper))

    loads[3].wait()
    tile = tile_ref[...]
    high_ref[0], low_ref[0] = split(tile)
    high_ref[1], low_ref[1] = split(jnp.transpose(tile))
    loads[2].wait()
    keep = jnp.where(d <= reach_ref[...], 1.0, 0.0) * jnp.where(r >= d, 1.0, 0.0)
    lone = jnp.where(off_diagonal, 0.0, 1.0)

    def multiply(sweep, mirror_half, far_vectors):
        mirror = []
        for part in range(halves):
            lanes = slice(part * span, part * span + span)
            mirror.append(mirror_half(lanes))
            for i in range(per_half):
                far_ref[sweep, part * per_half + i] = mirror[part][:, 128 * i : 128 * i + 128]

            @pl.when(off_diagonal)
            def _():
                if sweep == 0 and part == 0:
                    wait_for(slab_ref.at[1, pl.ds(0, chunks)], z_first_sem.at[1])
                for turn in range(per_half):
                    i = part * per_half + lax.rem(d + turn, per_half)
                    push(
                        far_ref.at[sweep, i],
                        parts_ref.at[sweep, n_col - 2 + d],
                        far_sent.at[sweep],
                        part_sem.at[sweep],
                        (j, owner(j, i)),
                    )

        pieces = split(far_vectors() * keep)
        for part in range(halves):
            lanes = slice(part * span, part * span + span)
            forward = dot_split(pieces, (high_ref[1, :, lanes], low_ref[1, :, lanes]), NN)
            forward = forward + lone * mirror[part]
            for i in range(per_half):
                own_ref[sweep, part * per_half + i] = forward[:, 128 * i : 128 * i + 128]
            for turn in range(per_half):
                i = part * per_half + lax.rem(c + turn, per_half)
                place = owner(r, i)

                @pl.when(c != place)
                def _():
                    push(
                        own_ref.at[sweep, i],
                        parts_ref.at[sweep, lax.rem(place - c + n_col, n_col) - 1],
                        own_sent.at[sweep],
                        part_sem.at[sweep],
                        (r, place),
                    )

    def total(sweep):
        wait_for(parts_ref.at[sweep], part_sem.at[sweep])
        return own_ref[sweep, mine] + jnp.sum(parts_ref[sweep], axis=0)

    side = jnp.where(off_diagonal, 1, 0)

    wait_for(slab_ref.at[0, pl.ds(0, n_col - 1)], z_row_sem)

    def far_pieces():
        @pl.when(off_diagonal)
        def _():
            wait_for(slab_ref.at[1, pl.ds(0, n_col - chunks)], z_first_sem.at[0])

        return slab_to_vectors(slab_ref[side])

    near = split(slab_to_vectors(slab_ref[0]) * keep)

    def first_half(lanes):
        return dot_split(near, (high_ref[0, :, lanes], low_ref[0, :, lanes]), NN)

    multiply(0, first_half, far_pieces)

    @pl.when(is_owner)
    def _():
        inside = mine == group

        @pl.when(inside)
        def _():
            wait_for(weight_parts_ref.at[pl.ds(0, 3)], weight_sem)

        @pl.when(jnp.logical_not(inside))
        def _():
            wait_for(weight_parts_ref, weight_sem)

        lane = iota((1, 128), 1) // SUB
        chunk_weight = sum(jnp.where(lane == i, weight_parts_ref[i], 0.0) for i in range(4))
        chunk_weight_ref[...] = chunk_weight
        values = total(0) * chunk_weight
        scaled = values * chunk_weight
        chunk_ref[...] = scaled
        wide_ref[0, mine] = scaled
        for o in peers:
            push(chunk_ref, wide_ref.at[0, mine], z_sent.at[1], z_near_sem.at[lax.div(mine, size)], peer(o))
        for o in users:
            push(chunk_ref, wide_ref.at[1, mine], z_sent.at[1], z_col_sem, user(o))
        gram_first_ref[...] = gram_spread(values)

    def near_part(part):
        own_part = jnp.logical_and(is_owner, lax.div(mine, size) == part)

        @pl.when(own_part)
        def _():
            if size > 1:
                wait_for(wide_ref.at[0, pl.ds(0, size - 1)], z_near_sem.at[part])

        @pl.when(jnp.logical_not(own_part))
        def _():
            wait_for(wide_ref.at[0, pl.ds(0, size)], z_near_sem.at[part])

        vectors = split(jnp.concatenate([wide_ref[0, size * part + i] for i in range(size)], axis=1) * keep)
        rows = pl.ds(pl.multiple_of(part * (128 * size), 128 * size), 128 * size)
        return lambda lanes: dot_split(vectors, (high_ref[0, rows, lanes], low_ref[0, rows, lanes]), NN)

    nearer = jnp.where(lax.div(c, y_count) == lax.div(home, y_count), 0, 1)
    product = near_part(nearer)
    early = [product(slice(part * span, part * span + span)) for part in range(halves)]
    product = near_part(1 - nearer)

    def second_half(lanes):
        return early[lanes.start // span] + product(lanes)

    def far_chunks():
        @pl.when(off_diagonal)
        def _():
            wait_for(wide_ref.at[1], z_col_sem)

        return jnp.concatenate([wide_ref[side, i] for i in range(chunks)], axis=1)

    multiply(1, second_half, far_chunks)

    @pl.when(is_owner)
    def _():
        values = total(1) * chunk_weight_ref[...]
        gram = rows_packed(gram_spread(values) + EPS * gram_first_ref[...], backward=True)
        gram_ref[0] = gram
        gram_row_ref[mine] = gram
        for o in peers:
            push(gram_ref.at[0], gram_row_ref.at[mine], gram_sent.at[0], gram_sem.at[0], peer(o))
        turned = jnp.transpose(jnp.concatenate([values] * 8, axis=0))
        result_ref[...] = rows_packed(turned).reshape(4, 4, 128)
        for i in range(4):
            place = 4 * mine + i

            @pl.when(c == place)
            def _():
                back_ref[...] = result_ref[i]

            @pl.when(c != place)
            def _():
                push(result_ref.at[i], back_ref, back_sent, back_sem, (r, place))

        if chunks > 1:
            wait_for(gram_row_ref.at[pl.ds(0, chunks - 1)], gram_sem.at[0])

    @pl.when(not_owner)
    def _():
        wait_for(gram_row_ref, gram_sem.at[0])

    gram_own = jnp.sum(gram_row_ref[...], axis=0)
    gram_ref[1] = gram_own
    for o in far_first(n_row, n_col):
        row = lax.rem(r + o, n_row)
        push(gram_ref.at[1], gram_col_ref.at[o - 1], gram_sent.at[1], gram_sem.at[1], (row, c))

    @pl.when(c != keeper)
    def _():
        wait_for(back_ref, back_sem)

    back = split(jnp.concatenate([back_ref[...]] * 4, axis=0))
    wait_for(slab_ref.at[:, pl.ds(0, n_col - 1)], z_sent.at[0])

    @pl.when(c != keeper)
    def _():
        wait_for(weight_row_ref, weight_sent)

    for sweep in range(2):

        @pl.when(off_diagonal)
        def _():
            wait_for(far_ref.at[sweep], far_sent.at[sweep])

        @pl.when(is_owner)
        def _():
            if chunks > 1:
                wait_for(own_ref.at[sweep, pl.ds(0, chunks - 1)], own_sent.at[sweep])

        @pl.when(not_owner)
        def _():
            wait_for(own_ref.at[sweep], own_sent.at[sweep])

    @pl.when(is_owner)
    def _():
        wait_for(parts_ref.at[0], z_sent.at[1])
        wait_for(gram_col_ref.at[pl.ds(0, n_col - 1)], gram_sent.at[0])

        @pl.when(mine == group)
        def _():
            wait_for(result_ref.at[pl.ds(0, 3)], back_sent)

        @pl.when(mine != group)
        def _():
            wait_for(result_ref, back_sent)

    wait_for(gram_col_ref, gram_sem.at[1])
    total_gram = gram_own + jnp.sum(gram_col_ref[...], axis=0)
    gram = jnp.concatenate(
        [
            pltpu.roll(jnp.broadcast_to(total_gram[i : i + 1], (8, 128)), K, 1, stride=K, stride_axis=0)
            for i in range(2)
        ],
        axis=0,
    )
    diagonal = jnp.where(iota((16, 128), 1) == iota((16, 128), 0), EPS * EPS, 0.0)
    solver = inverse_factor(gram * (1.0 / states) + diagonal)
    wide = jnp.concatenate([solver] * 8, axis=0)
    wide = jnp.where(iota((128, 128), 0) // K == iota((128, 128), 1) // K, wide, 0.0)
    out_ref[...] = dot_split(back, split(wide), NT)[0:4]
    wait_for(gram_col_ref, gram_sent.at[1])


def local(start_modes, tiles, reach, weights, n_row, n_col):
    width = tiles.shape[-1]
    chunks = n_col // 4
    dma = pltpu.SemaphoreType.DMA
    out = pl.pallas_call(
        functools.partial(kernel, n_row, n_col, n_row * width),
        out_shape=pltpu.VMEM((4, 128), F32),
        in_specs=[pl.BlockSpec(memory_space=pltpu.HBM)] * 4,
        out_specs=pl.BlockSpec(memory_space=pltpu.VMEM),
        scratch_shapes=[
            pltpu.VMEM((4, 128), F32),
            pltpu.VMEM((width, width), F32),
            pltpu.VMEM((1, 1), jnp.int32),
            pltpu.VMEM((1, SUB), F32),
            pltpu.VMEM((2, width, width), BF16),
            pltpu.VMEM((2, width, width), BF16),
            pltpu.VMEM((1, 128), F32),
            pltpu.VMEM((4, 1, 128), F32),
            pltpu.VMEM((1, 128), F32),
            pltpu.VMEM((4, 128), F32),
            pltpu.VMEM((2, n_col, 4, 128), F32),
            pltpu.VMEM((2, chunks, K, 128), F32),
            pltpu.VMEM((2, chunks, K, 128), F32),
            pltpu.VMEM((2, 2 * (n_col - 1), K, 128), F32),
            pltpu.VMEM((K, 128), F32),
            pltpu.VMEM((2, chunks, K, 128), F32),
            pltpu.VMEM((K, 128), F32),
            pltpu.VMEM((2, 2, 128), F32),
            pltpu.VMEM((chunks, 2, 128), F32),
            pltpu.VMEM((n_row - 1, 2, 128), F32),
            pltpu.VMEM((4, 4, 128), F32),
            pltpu.VMEM((4, 128), F32),
            dma((4,)),
            dma(()),
            dma(()),
            dma((2,)),
            dma((2,)),
            dma(()),
            dma((2,)),
            dma((2,)),
            dma(()),
            dma(()),
            dma((2,)),
            dma((2,)),
            dma((2,)),
            dma((2,)),
            dma(()),
        ],
        compiler_params=pltpu.CompilerParams(
            collective_id=0, has_side_effects=True, vmem_limit_bytes=60 * 1024 * 1024
        ),
    )(
        start_modes.reshape(4, 128),
        tiles.reshape(width, width),
        reach,
        weights.reshape(1, SUB),
    )
    return out.reshape(start_modes.shape)


def solution(mesh):
    return jax.shard_map(
        functools.partial(local, n_row=mesh.shape["trow"], n_col=mesh.shape["tcol"]),
        mesh=mesh,
        in_specs=(
            P(None, "trow", "tcol", None),
            P(None, "trow", "tcol", None, None, None),
            P(None, "trow"),
            P(None, "trow", "tcol", None),
        ),
        out_specs=P(None, "trow", "tcol", None),
        check_vma=False,
    )
```
